128 devices in a mesh: rep: 2 (over y_hi), shard: 64 (over z, x, y_lo, core).
Axes of the slice: x: 4, y: 4 (y_hi: 2, y_lo: 2; y = y_hi * 2 + y_lo), z: 4, core: 2. Of those that a mesh axis runs over, the one named last changes fastest.
Arguments:
- tokens: bfloat16 [32768, 1024], P(('rep', 'shard')), may hold values from -6 to 6
- cotangent: bfloat16 [32768, 1024], P(('rep', 'shard')), may hold values from -6 to 6
- seq_lengths: int32 [512], replicated, may hold values from 0 to 256, as said below
- seq_device: int32 [512], replicated, may hold values from 0 to 127, as said below
- in_weight: float32 [1024, 3072], P('shard'), may hold values from -0.1875 to 0.1875
- conv_kernel: float32 [1024, 3], P('shard'), may hold values from -3.5 to 3.5
- out_weight: float32 [1024, 1024], P('shard'), may hold values from -0.1875 to 0.1875
- norm_gain: float32 [1024], P('shard'), may hold values from 0.5 to 1.5
- gate_weight: float32 [1024, 4608], P('shard'), may hold values from -0.1875 to 0.1875
- up_weight: float32 [1024, 4608], P('shard'), may hold values from -0.1875 to 0.1875
- down_weight: float32 [4608, 1024], P('shard'), may hold values from -0.09375 to 0.09375
- moment_in: float32 [1024, 3072], P('shard'), may hold values from -96 to 96
- moment_conv: float32 [1024, 3], P('shard'), may hold values from -128 to 128
- moment_out: float32 [1024, 1024], P('shard'), may hold values from -96 to 96
- moment_gain: float32 [1024], P('shard'), may hold values from -96 to 96
- moment_gate: float32 [1024, 4608], P('shard'), may hold values from -32 to 32
- moment_up: float32 [1024, 4608], P('shard'), may hold values from -32 to 32
- moment_down: float32 [4608, 1024], P('shard'), may hold values from -64 to 64
- square_in: float32 [1024, 3072], P('shard'), may hold values from 1310.72 to 5242.88
- square_conv: float32 [1024, 3], P('shard'), may hold values from 1900.544 to 7536.64
- square_out: float32 [1024, 1024], P('shard'), may hold values from 1310.72 to 5242.88
- square_gain: float32 [1024], P('shard'), may hold values from 1048.576 to 4259.84
- square_gate: float32 [1024, 4608], P('shard'), may hold values from 117.9648 to 471.8592
- square_up: float32 [1024, 4608], P('shard'), may hold values from 117.9648 to 471.8592
- square_down: float32 [4608, 1024], P('shard'), may hold values from 471.8592 to 1900.544
Outputs:
- block_out: bfloat16 [32768, 1024], P(('rep', 'shard'))
- input_grad: float32 [32768, 1024], P(('rep', 'shard'))
- updated_in: float32 [1024, 3072], P('shard')
- updated_conv: float32 [1024, 3], P('shard')
- updated_out: float32 [1024, 1024], P('shard')
- updated_gain: float32 [1024], P('shard')
- updated_gate: float32 [1024, 4608], P('shard')
- updated_up: float32 [1024, 4608], P('shard')
- updated_down: float32 [4608, 1024], P('shard')
- first_in: float32 [1024, 3072], P('shard')
- first_conv: float32 [1024, 3], P('shard')
- first_out: float32 [1024, 1024], P('shard')
- first_gain: float32 [1024], P('shard')
- first_gate: float32 [1024, 4608], P('shard')
- first_up: float32 [1024, 4608], P('shard')
- first_down: float32 [4608, 1024], P('shard')
- second_in: float32 [1024, 3072], P('shard')
- second_conv: float32 [1024, 3], P('shard')
- second_out: float32 [1024, 1024], P('shard')
- second_gain: float32 [1024], P('shard')
- second_gate: float32 [1024, 4608], P('shard')
- second_up: float32 [1024, 4608], P('shard')
- second_down: float32 [4608, 1024], P('shard')
The draws below stay inside these ranges and needn't reach their ends.
Inputs may be any that keep to these rules, and one draw needn't show every extreme that they name: `seq_lengths`: the lengths of the entries of one device sum to between 128 and 256; a length of 0 marks an unused entry; some device holds a single sequence of 256 rows. `seq_device`: every device is named by exactly 4 entries.
All inputs are finite; a program needn't handle non-finite values.
Results may differ from the reference program's by a relative error of at most 0.011.
Values may be sent and summed in bfloat16 or wider, within the bound.
No kernel may reach another device: no remote copies, remote signals or barrier semaphores. Data moves between devices by JAX's collectives and lax.ppermute only.
A program may use at most 256 MiB of HBM per device.

```python
import math
import jax
import jax.numpy as jnp
from jax import lax

D = 1024
FF = 4608
KW = 3
STEP = 10
TOK_DEV = 256
SEQ_DEV = 4
TOKENS = 32768
SEQS = 512
N_REP = 2
N_SHARD = 64


def deal_sequences(key):
    device_count = N_REP * N_SHARD
    key_total, key_cut, key_pick, key_order = jax.random.split(key, 4)
    device_ids = jnp.arange(device_count, dtype=jnp.int32)
    totals = jax.random.randint(key_total, (device_count,), TOK_DEV // 2, TOK_DEV + 1, dtype=jnp.int32)
    chosen = jax.random.randint(key_pick, (), 0, device_count, dtype=jnp.int32)
    totals = jnp.where(device_ids == chosen, TOK_DEV, totals)
    cuts = jax.random.randint(key_cut, (device_count, SEQ_DEV - 1), 0, TOK_DEV + 1, dtype=jnp.int32)
    cuts = jnp.minimum(cuts, totals[:, None])
    cuts = jnp.where((device_ids == chosen)[:, None], 0, cuts)
    starts = jnp.zeros((device_count, 1), jnp.int32)
    bounds = jnp.sort(jnp.concatenate([starts, cuts, totals[:, None]], axis=1), axis=1)
    lengths = (bounds[:, 1:] - bounds[:, :-1]).reshape(-1)
    owners = jnp.repeat(device_ids, SEQ_DEV)
    placing = jax.random.permutation(key_order, device_count * SEQ_DEV)
    flat_lengths = jnp.zeros((device_count * SEQ_DEV,), jnp.int32).at[placing].set(lengths)
    flat_owners = jnp.zeros((device_count * SEQ_DEV,), jnp.int32).at[placing].set(owners)
    return (flat_lengths, flat_owners)


def draw_seq_lengths(key, part):
    return deal_sequences(key)[0]


def draw_seq_device(key, part):
    return deal_sequences(key)[1]


def steps_of(key, shape, cuts, low, high):
    factor_of, own = 1.0, jax.random.fold_in(key, 6)
    for position, parts in cuts:
        steps = jnp.exp(jax.random.uniform(jax.random.fold_in(own, position), (parts,), jnp.float32, low / len(cuts), high / len(cuts)))
        factor_of = factor_of * jnp.repeat(steps, shape[position] // parts).reshape([-1 if axis == position else 1 for axis in range(len(shape))])
    return factor_of


def noise(own_key, shape, width, most, cuts=(), kind=jnp.bfloat16):
    entries = jax.random.normal(own_key, shape, jnp.float32) * width
    if len(cuts) > 0:
        entries = steps_of(own_key, shape, cuts, -0.22, 0.18) * entries
    return jnp.clip(entries, min=-most, max=most).astype(kind)


def setup_inputs(seed: int = 0) -> dict:
    key_of = jax.random.split(jax.random.key(seed), 26)
    tokens = noise(key_of[0], (TOKENS, D), 1.0, 6.0, ((0, 128),))
    cotangent = noise(key_of[1], (TOKENS, D), 1.0, 6.0, ((0, 128),))
    seq_lengths = draw_seq_lengths(jax.random.fold_in(key_of[25], 71), 0)
    seq_device = draw_seq_device(jax.random.fold_in(key_of[25], 71), 0)
    in_weight = noise(key_of[4], (D, 3 * D), D ** -0.5, 0.1875, ((0, 64),), jnp.float32)
    conv_kernel = noise(key_of[5], (D, KW), 0.6, 3.5, ((0, 64),), jnp.float32)
    out_weight = noise(key_of[6], (D, D), D ** -0.5, 0.1875, ((0, 64),), jnp.float32)
    norm_gain = jnp.clip(1.0 + 0.1 * jax.random.normal(key_of[7], (D,), jnp.float32), 0.5, 1.5)
    gate_weight = noise(key_of[8], (D, FF), D ** -0.5, 0.1875, ((0, 64),), jnp.float32)
    up_weight = noise(key_of[9], (D, FF), D ** -0.5, 0.1875, ((0, 64),), jnp.float32)
    down_weight = noise(key_of[10], (FF, D), FF ** -0.5, 0.09375, ((0, 64),), jnp.float32)
    moment_in = noise(key_of[11], (D, 3 * D), (0.095 * TOKENS ** 0.5), 96.0, ((0, 64),), jnp.float32)
    moment_conv = noise(key_of[12], (D, KW), (0.11 * TOKENS ** 0.5), 128.0, ((0, 64),), jnp.float32)
    moment_out = noise(key_of[13], (D, D), (0.095 * TOKENS ** 0.5), 96.0, ((0, 64),), jnp.float32)
    moment_gain = noise(key_of[14], (D,), (0.085 * TOKENS ** 0.5), 96.0, ((0, 64),), jnp.float32)
    moment_gate = noise(key_of[15], (D, FF), (0.03 * TOKENS ** 0.5), 32.0, ((0, 64),), jnp.float32)
    moment_up = noise(key_of[16], (D, FF), (0.03 * TOKENS ** 0.5), 32.0, ((0, 64),), jnp.float32)
    moment_down = noise(key_of[17], (FF, D), (0.057 * TOKENS ** 0.5), 64.0, ((0, 64),), jnp.float32)
    square_in = jnp.clip(jnp.exp(math.log(5242.88) - 1.3862944 * jax.random.uniform(key_of[18], (D, 3 * D), jnp.float32) ** steps_of(key_of[18], (D, 3 * D), ((0, 64),), -0.2, 0.2)), 1310.72, 5242.88)
    square_conv = jnp.clip(jnp.exp(math.log(7536.64) - 1.3776363 * jax.random.uniform(key_of[19], (D, KW), jnp.float32) ** steps_of(key_of[19], (D, KW), ((0, 64),), -0.2, 0.2)), 1900.544, 7536.64)
    square_out = jnp.clip(jnp.exp(math.log(5242.88) - 1.3862944 * jax.random.uniform(key_of[20], (D, D), jnp.float32) ** steps_of(key_of[20], (D, D), ((0, 64),), -0.2, 0.2)), 1310.72, 5242.88)
    square_gain = jnp.clip(jnp.exp(math.log(4259.84) - 1.4017985 * jax.random.uniform(key_of[21], (D,), jnp.float32) ** steps_of(key_of[21], (D,), ((0, 64),), -0.2, 0.2)), 1048.576, 4259.84)
    square_gate = jnp.clip(jnp.exp(math.log(471.8592) - 1.3862944 * jax.random.uniform(key_of[22], (D, FF), jnp.float32) ** steps_of(key_of[22], (D, FF), ((0, 64),), -0.2, 0.2)), 117.9648, 471.8592)
    square_up = jnp.clip(jnp.exp(math.log(471.8592) - 1.3862944 * jax.random.uniform(key_of[23], (D, FF), jnp.float32) ** steps_of(key_of[23], (D, FF), ((0, 64),), -0.2, 0.2)), 117.9648, 471.8592)
    square_down = jnp.clip(jnp.exp(math.log(1900.544) - 1.3932148 * jax.random.uniform(key_of[24], (FF, D), jnp.float32) ** steps_of(key_of[24], (FF, D), ((0, 64),), -0.2, 0.2)), 471.8592, 1900.544)
    return {"tokens": tokens, "cotangent": cotangent, "seq_lengths": seq_lengths, "seq_device": seq_device, "in_weight": in_weight, "conv_kernel": conv_kernel, "out_weight": out_weight, "norm_gain": norm_gain, "gate_weight": gate_weight, "up_weight": up_weight, "down_weight": down_weight, "moment_in": moment_in, "moment_conv": moment_conv, "moment_out": moment_out, "moment_gain": moment_gain, "moment_gate": moment_gate, "moment_up": moment_up, "moment_down": moment_down, "square_in": square_in, "square_conv": square_conv, "square_out": square_out, "square_gain": square_gain, "square_gate": square_gate, "square_up": square_up, "square_down": square_down}


NORM_EPS = 1e-05
BETA_ONE = 0.9
BETA_TWO = 0.95
ADAM_EPS = 1e-08
STEP_RATES = (0.02, 0.3, 0.02, 0.3, 0.02, 0.02, 0.02)
DECAY_RATES = (0.1, 0.0, 0.1, 0.0, 0.1, 0.1, 0.1)

@jax.custom_vjp
def low(v):
    return lax.optimization_barrier(v.astype(jnp.bfloat16)).astype(jnp.float32)

@jax.custom_vjp
def low_back(v):
    return v

def low_keep(v):
    return (low(v), None)

def low_pass(kept, grad):
    return (grad,)

def back_keep(v):
    return (v, None)

def back_low(kept, grad):
    return (low(grad),)
low.defvjp(low_keep, low_pass)
low_back.defvjp(back_keep, back_low)

def layout(seq_lengths, seq_device, device, row_count):
    owned_len = jnp.where(seq_device == device, seq_lengths, 0).astype(jnp.int32)
    seq_ends = jnp.cumsum(owned_len, dtype=jnp.int32)
    slot_index = jnp.arange(row_count, dtype=jnp.int32)
    segment = lax.optimization_barrier(jnp.sum((seq_ends[None, :] <= slot_index[:, None]).astype(jnp.int32), axis=1, dtype=jnp.int32))
    live_rows = (slot_index < seq_ends[-1]).astype(jnp.int32)
    return (segment, live_rows)

def matmul(left, right):
    return jnp.dot(left, right, precision=lax.Precision.HIGHEST)

def causal_conv(mixed, kernel, segment):
    summed = mixed * kernel[:, 0]
    for offset in range(1, KW):
        earlier = jnp.pad(mixed, ((offset, 0), (0, 0)))[:-offset]
        before = jnp.pad(segment, (offset, 0), constant_values=-1)[:-offset]
        summed = summed + jnp.where((before == segment)[:, None], earlier * kernel[:, offset], 0.0)
    return summed

def block_forward(params, inputs, segment, live_rows):
    in_w, kernel, out_w, gain, gate_w, up_w, down_w = [low(weight) for weight in params]
    model_width = in_w.shape[0]
    projected = low_back(matmul(low(inputs), in_w))
    b_branch = projected[:, :model_width]
    c_branch = projected[:, model_width:2 * model_width]
    x_branch = projected[:, 2 * model_width:]
    convolved = causal_conv(b_branch * x_branch, kernel, segment)
    mixer_out = low_back(matmul(low(c_branch * convolved), out_w))
    hidden = inputs + mixer_out
    inv_rms = lax.rsqrt(lax.optimization_barrier(jnp.mean(hidden * hidden, axis=-1, keepdims=True)) + NORM_EPS)
    normed = low(hidden * inv_rms * gain)
    gate_pre = low_back(matmul(normed, gate_w))
    up_pre = low_back(matmul(normed, up_w))
    act_low = low(jax.nn.silu(gate_pre) * up_pre)
    ffn_out = low_back(matmul(act_low, down_w))
    return (hidden + ffn_out) * live_rows[:, None]

def reference(tokens, cotangent, seq_lengths, seq_device, in_weight, conv_kernel, out_weight, norm_gain, gate_weight, up_weight, down_weight, moment_in, moment_conv, moment_out, moment_gain, moment_gate, moment_up, moment_down, square_in, square_conv, square_out, square_gain, square_gate, square_up, square_down):
    device_count = N_REP * N_SHARD
    params = (in_weight, conv_kernel, out_weight, norm_gain, gate_weight, up_weight, down_weight)
    moments = (moment_in, moment_conv, moment_out, moment_gain, moment_gate, moment_up, moment_down)
    squares = (square_in, square_conv, square_out, square_gain, square_gate, square_up, square_down)
    device_ids = jnp.arange(device_count, dtype=jnp.int32)

    def device_layout(device):
        return layout(seq_lengths, seq_device, device, TOK_DEV)
    segment, live_rows = jax.vmap(device_layout)(device_ids)
    segment = (segment + device_ids[:, None] * (SEQS + 1)).astype(jnp.int32)
    group_size = math.gcd(device_count, max(1, 4096 // TOK_DEV))
    group_count = device_count // group_size
    row_count = group_size * TOK_DEV
    model_width = tokens.shape[1]
    blocks = (tokens.reshape(group_count, row_count, model_width), cotangent.reshape(group_count, row_count, model_width), segment.reshape(group_count, row_count), live_rows.reshape(group_count, row_count).astype(jnp.float32))

    def one_group(running, block):
        inputs, incoming, seg_block, live_block = block

        def forward(weights, values):
            return block_forward(weights, values, seg_block, live_block)
        result, pullback = jax.vjp(forward, params, inputs.astype(jnp.float32))
        weight_grads, input_grads = pullback(incoming.astype(jnp.float32))
        running = tuple((acc + part for acc, part in zip(running, weight_grads)))
        return (running, (result.astype(jnp.bfloat16), input_grads))
    zero_grads = tuple((jnp.zeros_like(weight) for weight in params))
    gradients, (outputs, input_grads) = lax.scan(one_group, zero_grads, blocks)
    bias_one = 1.0 - BETA_ONE ** STEP
    bias_two = 1.0 - BETA_TWO ** STEP
    updated = []
    firsts = []
    seconds = []
    for master, moment, variance, gradient, step_rate, decay_rate in zip(params, moments, squares, gradients, STEP_RATES, DECAY_RATES):
        first_new = BETA_ONE * moment + (1.0 - BETA_ONE) * gradient
        second_new = BETA_TWO * variance + (1.0 - BETA_TWO) * gradient * gradient
        normalized = first_new / bias_one / (jnp.sqrt(second_new / bias_two) + ADAM_EPS)
        updated.append(master - step_rate * (normalized + decay_rate * master))
        firsts.append(first_new)
        seconds.append(second_new)
    block_out = outputs.reshape(TOKENS, model_width)
    input_grad = input_grads.reshape(TOKENS, model_width)
    return (block_out, input_grad, updated[0], updated[1], updated[2], updated[3], updated[4], updated[5], updated[6], firsts[0], firsts[1], firsts[2], firsts[3], firsts[4], firsts[5], firsts[6], seconds[0], seconds[1], seconds[2], seconds[3], seconds[4], seconds[5], seconds[6])
```

```python
import jax
import jax.numpy as jnp
from jax import lax
from jax.experimental import pallas as pl
from jax.experimental.pallas import tpu as pltpu
from jax.sharding import Mesh
from jax.sharding import PartitionSpec as P

STEP = 10
NORM_EPS = 1e-05
BETA_ONE = 0.9
BETA_TWO = 0.95
ADAM_EPS = 1e-08
STEP_RATES = (0.02, 0.3, 0.02, 0.3, 0.02, 0.02, 0.02)
DECAY_RATES = (0.1, 0.0, 0.1, 0.0, 0.1, 0.1, 0.1)

AXES = ("rep", "z", "x", "y", "core")
SHARD = ("z", "x", "y", "core")
SIDE = 4
AUX = 128


def layout(seq_lengths, seq_device, device, row_count):
    owned_len = jnp.where(seq_device == device, seq_lengths, 0)
    seq_ends = jnp.cumsum(owned_len, dtype=jnp.int32)
    slot_index = jnp.arange(row_count, dtype=jnp.int32)
    segment = jnp.sum(
        (seq_ends[None, :] <= slot_index[:, None]).astype(jnp.int32), axis=1, dtype=jnp.int32
    )
    live_rows = (slot_index < seq_ends[-1]).astype(jnp.int32)
    return (segment, live_rows)


def product(left, right):
    return jnp.dot(left, right, preferred_element_type=jnp.float32)


def product_nt(left, right):
    return lax.dot_general(
        left, right, (((1,), (1,)), ((), ())), preferred_element_type=jnp.float32
    )


def product_tn(left, right):
    return lax.dot_general(
        left, right, (((0,), (0,)), ((), ())), preferred_element_type=jnp.float32
    )


def conv_forward(mixed, taps, segment):
    summed = mixed * taps[0]
    matches = []
    for offset in range(1, len(taps)):
        earlier = jnp.pad(mixed, ((offset, 0), (0, 0)))[:-offset]
        same_seq = (jnp.pad(segment, (offset, 0), constant_values=-1)[:-offset] == segment)[:, None]
        matches.append(same_seq)
        summed = summed + jnp.where(same_seq, earlier * taps[offset], 0.0)
    return (summed, matches)


def conv_backward(gradient, mixed, taps, matches):
    grad_mixed = gradient * taps[0]
    grad_taps = [jnp.sum(gradient * mixed, axis=0)]
    for offset in range(1, len(taps)):
        masked = jnp.where(matches[offset - 1], gradient, 0.0)
        later = jnp.pad(masked, ((0, offset), (0, 0)))[offset:]
        grad_mixed = grad_mixed + later * taps[offset]
        earlier = jnp.pad(mixed, ((offset, 0), (0, 0)))[:-offset]
        grad_taps.append(jnp.sum(masked * earlier, axis=0))
    return (grad_mixed, grad_taps)


def low(value):
    return value.astype(jnp.bfloat16)


def wide(value):
    return value.astype(jnp.float32)


def after(value, *earlier):
    return lax.optimization_barrier((value,) + earlier)[0]


def plane_shift(value, distance, turn):
    pairs = []
    for z in range(SIDE):
        for x in range(SIDE):
            for core in range(2):
                if (core + turn) % 2 == 0:
                    to_z, to_x = z, (x + distance) % SIDE
                else:
                    to_z, to_x = (z + distance) % SIDE, x
                pairs.append(((z * SIDE + x) * 2 + core, (to_z * SIDE + to_x) * 2 + core))
    return lax.ppermute(value, ("z", "x", "core"), pairs)


def ring_shift(value, distance, swap=0):
    pairs = []
    for y in range(SIDE):
        for core in range(2):
            pairs.append((y * 2 + core, (y + distance) % SIDE * 2 + (core + swap) % 2))
    return lax.ppermute(value, ("rep", "y", "core"), pairs)


def core_swap(value):
    return lax.ppermute(value, "core", [(0, 1), (1, 0)])


def pair_swap(value):
    return lax.ppermute(value, "y", [(0, 1), (1, 0)])


def in_order(index, mine, other):
    first = jnp.where(index == 0, mine, other)
    second = jnp.where(index == 0, other, mine)
    return jnp.concatenate([first, second], axis=0)


def any_specs(count):
    return [pl.BlockSpec(memory_space=pl.ANY)] * count


def move_blocks(sources, out_shapes, index, moves):
    count = len(sources)

    def kernel(index_ref, *refs):
        sems = refs[-1]
        ins, outs = refs[:count], refs[count:-1]
        copies = [
            pltpu.make_async_copy(source, target, sems.at[i])
            for i, (source, target) in enumerate(moves(ins, outs, index_ref))
        ]
        for copy in copies:
            copy.start()
        for copy in copies:
            copy.wait()

    total = sum(1 for _ in moves_count(moves, sources, out_shapes))
    moved = sum(s.size * s.dtype.itemsize for s in out_shapes)
    return pl.pallas_call(
        kernel,
        out_shape=out_shapes,
        in_specs=[pl.BlockSpec(memory_space=pltpu.SMEM)] + any_specs(count),
        out_specs=any_specs(len(out_shapes)),
        scratch_shapes=[pltpu.SemaphoreType.DMA((total,))],
        cost_estimate=pl.CostEstimate(flops=0, bytes_accessed=2 * moved, transcendentals=0),
    )(index, *sources)


class Blank:
    @property
    def at(self):
        return self

    def __getitem__(self, key):
        return self


def moves_count(moves, sources, out_shapes):
    class Index:
        def __getitem__(self, key):
            return 0

    return list(moves([Blank()] * len(sources), [Blank()] * len(out_shapes), Index()))


def gather_plane(block):
    first = [block] + [plane_shift(block, d, 0) for d in (1, 2, 3)]
    joined = jnp.concatenate(first, axis=0)
    return [joined] + [plane_shift(joined, d, 1) for d in (1, 2, 3)]


def plane_places(z, x, core):
    places = []
    for d2 in range(SIDE):
        for d1 in range(SIDE):
            at_z = jnp.where(core == 0, (z - d2) % SIDE, (z - d1) % SIDE)
            at_x = jnp.where(core == 0, (x - d1) % SIDE, (x - d2) % SIDE)
            places.append(at_z * SIDE + at_x)
    return jnp.stack(places).astype(jnp.int32)


def plane_sources(z, x, core):
    picks = []
    for d in range(SIDE):
        for k in range(SIDE):
            at_z = jnp.where(core == 0, (z + d) % SIDE, k)
            at_x = jnp.where(core == 0, k, (x + d) % SIDE)
            picks.append(at_z * SIDE + at_x)
    return jnp.stack(picks).astype(jnp.int32)


def sum_wide(parts):
    total = wide(parts[0])
    for part in parts[1:]:
        total = total + wide(part)
    return total


def reduce_plane(blocks, z, x, core):
    rows, columns = blocks.shape[1:]
    shape = jax.ShapeDtypeStruct((SIDE, rows, columns), blocks.dtype)

    def moves(ins, outs, index):
        for d in range(SIDE):
            for k in range(SIDE):
                yield ins[0].at[index[d * SIDE + k]], outs[d].at[k]

    messages = move_blocks([blocks], [shape] * SIDE, plane_sources(z, x, core), moves)
    parts = [messages[0]] + [plane_shift(messages[d], d, 1) for d in (1, 2, 3)]
    summed = low(sum_wide(parts))
    me = jnp.where(core == 0, x, z)
    pick = lambda d: lax.dynamic_index_in_dim(summed, (me + d) % SIDE, 0, keepdims=False)
    return low(sum_wide([pick(0)] + [plane_shift(pick(d), d, 0) for d in (1, 2, 3)]))


def reduce_ring(pair, y):
    own = lax.dynamic_index_in_dim(pair, y, 0, keepdims=False)
    other = lax.dynamic_index_in_dim(pair, 1 - y, 0, keepdims=False)
    return sum_wide([own, ring_shift(other, 1), ring_shift(other, 3), ring_shift(own, 2)])


def body(
    tokens,
    cotangent,
    seq_lengths,
    seq_device,
    in_weight,
    conv_kernel,
    out_weight,
    norm_gain,
    gate_weight,
    up_weight,
    down_weight,
    moment_in,
    moment_conv,
    moment_out,
    moment_gain,
    moment_gate,
    moment_up,
    moment_down,
    square_in,
    square_conv,
    square_out,
    square_gain,
    square_gate,
    square_up,
    square_down,
):
    masters = (in_weight, conv_kernel, out_weight, norm_gain, gate_weight, up_weight, down_weight)
    moments = (moment_in, moment_conv, moment_out, moment_gain, moment_gate, moment_up, moment_down)
    squares = (square_in, square_conv, square_out, square_gain, square_gate, square_up, square_down)
    rep, z, x, y, core = [lax.axis_index(name) for name in AXES]
    device = (((rep * SIDE + z) * SIDE + x) * 2 + y) * 2 + core
    slots, width = tokens.shape
    rows = in_weight.shape[0]
    hidden_units = gate_weight.shape[1]
    half = hidden_units // 2
    down_rows = down_weight.shape[0]
    chips = SIDE * SIDE
    tap_count = conv_kernel.shape[1]
    in_columns = in_weight.shape[1]
    mix_columns = in_columns + width + AUX

    segment, live_rows = layout(seq_lengths, seq_device, device, slots)
    live_float = wide(live_rows)[:, None]
    places = plane_places(z, x, core)

    small = jnp.concatenate([conv_kernel, norm_gain[:, None]], axis=1)
    small = jnp.pad(low(small), ((0, 0), (0, AUX - tap_count - 1)))
    mix_local = jnp.concatenate([low(in_weight), low(out_weight), small], axis=1)
    mix_pair = in_order(y, mix_local, pair_swap(mix_local))
    mix_first = [mix_pair] + [plane_shift(mix_pair, d, 0) for d in (1, 2, 3)]
    mix_joined = jnp.concatenate(mix_first, axis=0)
    mix_own = [mix_joined] + [plane_shift(mix_joined, d, 1) for d in (1, 2, 3)]
    mix_other = [core_swap(part) for part in mix_own]
    other_places = plane_places(z, x, 1 - core)
    parts = [part.reshape(SIDE, 2, rows, mix_columns) for part in mix_own + mix_other]

    def mix_moves(ins, outs, index):
        bounds = [(0, in_columns), (in_columns, width), (in_columns + width, AUX)]
        for side in range(2):
            where = index[2 * chips + side]
            for d2 in range(SIDE):
                for d1 in range(SIDE):
                    place = index[side * chips + d2 * SIDE + d1]
                    for out, (start, size) in zip(outs, bounds):
                        source = ins[side * SIDE + d2].at[d1, :, :, pl.ds(start, size)]
                        yield source, out.at[place, :, where]

    both = jnp.stack([core, 1 - core]).astype(jnp.int32)
    mix_index = jnp.concatenate([places, other_places, both])
    in_w, out_w, small_w = move_blocks(
        parts,
        [
            jax.ShapeDtypeStruct((chips, 2, 2, rows, columns), jnp.bfloat16)
            for columns in (in_columns, width, AUX)
        ],
        mix_index,
        mix_moves,
    )
    in_w = in_w.reshape(width, in_columns)
    out_w = out_w.reshape(width, width)
    small_w = wide(small_w.reshape(width, AUX)[:, : tap_count + 1]).T
    taps = [small_w[k] for k in range(tap_count)]
    gain = small_w[tap_count]

    def by_core(weight):
        return low(weight).reshape(rows, -1, 2, down_rows)

    gate_split, up_split = by_core(gate_weight), by_core(up_weight)
    unit_halves = [
        jnp.concatenate(
            [gate_split[:, :, c].reshape(rows, half), up_split[:, :, c].reshape(rows, half)], axis=1
        )
        for c in range(2)
    ]
    mine = jnp.where(core == 0, unit_halves[0], unit_halves[1])
    theirs = jnp.where(core == 0, unit_halves[1], unit_halves[0])
    unit_pair = in_order(core, mine, core_swap(theirs))
    unit_pair = after(unit_pair, *mix_first)
    unit_first = [unit_pair] + [plane_shift(unit_pair, d, 0) for d in (1, 2, 3)]
    unit_joined = after(jnp.concatenate(unit_first, axis=0), *mix_own)
    unit_own = [unit_joined] + [plane_shift(unit_joined, d, 1) for d in (1, 2, 3)]
    unit_other = [ring_shift(part, 1 if i < 2 else 3) for i, part in enumerate(unit_own)]
    parts = [part.reshape(SIDE, 2 * rows, 2 * half) for part in unit_own + unit_other]

    def unit_moves(ins, outs, index):
        for side in range(2):
            where = index[chips + side]
            for d2 in range(SIDE):
                for d1 in range(SIDE):
                    place = index[d2 * SIDE + d1]
                    yield ins[side * SIDE + d2].at[d1], outs[0].at[place, where]

    unit_index = jnp.concatenate([places, jnp.stack([y, 1 - y]).astype(jnp.int32)])
    (unit_w,) = move_blocks(
        parts,
        [jax.ShapeDtypeStruct((chips, 2, 2 * rows, 2 * half), jnp.bfloat16)],
        unit_index,
        unit_moves,
    )
    unit_w = unit_w.reshape(width, 2 * half)

    down_low = low(down_weight)
    down_pair = in_order(y, down_low, pair_swap(down_low))
    down_pair = after(down_pair, *unit_first)
    down_first = [down_pair] + [plane_shift(down_pair, d, 0) for d in (1, 2, 3)]
    down_joined = after(jnp.concatenate(down_first, axis=0), *unit_own)
    down_own = [down_joined] + [plane_shift(down_joined, d, 1) for d in (1, 2, 3)]
    parts = [part.reshape(SIDE, 2 * down_rows, width) for part in down_own]

    def down_moves(ins, outs, index):
        for d2 in range(SIDE):
            for d1 in range(SIDE):
                yield ins[d2].at[d1], outs[0].at[index[d2 * SIDE + d1]]

    (down_w,) = move_blocks(
        parts,
        [jax.ShapeDtypeStruct((chips, 2 * down_rows, width), jnp.bfloat16)],
        places,
        down_moves,
    )
    down_w = down_w.reshape(half, width)

    projected = product(tokens, in_w)
    b_branch = projected[:, :width]
    c_branch = projected[:, width : 2 * width]
    x_branch = projected[:, 2 * width :]
    mixed = b_branch * x_branch
    convolved, matches = conv_forward(mixed, taps, segment)
    conv_low = low(c_branch * convolved)
    hidden = wide(tokens) + product(conv_low, out_w)
    inv_rms = lax.rsqrt(jnp.mean(hidden * hidden, axis=-1, keepdims=True) + NORM_EPS)
    scaled = hidden * inv_rms
    normed = low(scaled * gain)

    grad_out = wide(cotangent) * live_float
    grad_low = low(grad_out)
    grad_both = jnp.concatenate([grad_low, core_swap(grad_low)], axis=0)
    normed_both = jnp.concatenate([normed, core_swap(normed)], axis=0)
    pre = product(normed_both, unit_w)
    gate_pre, up_pre = pre[:, :half], pre[:, half:]
    sigmoid_gate = jax.nn.sigmoid(gate_pre)
    silu_gate = gate_pre * sigmoid_gate
    act_low = low(silu_gate * up_pre)
    ffn_part = product(act_low, down_w)
    grad_act = product_nt(grad_both, down_w)
    grad_down = low(product_tn(act_low, grad_both))
    grad_up = low(grad_act * silu_gate)
    grad_gate = low(grad_act * up_pre * sigmoid_gate * (1.0 + gate_pre * (1.0 - sigmoid_gate)))
    grad_pre = jnp.concatenate([grad_gate, grad_up], axis=1)
    norm_part = product_nt(grad_pre, unit_w)
    grad_norm = norm_part[:slots] + wide(core_swap(low(norm_part[slots:])))
    ffn_out = ffn_part[:slots] + wide(core_swap(low(ffn_part[slots:])))
    block_out = low((hidden + ffn_out) * live_float)
    grad_unit = low(product_tn(normed_both, grad_pre)).reshape(chips, 2, 2 * rows, 2 * half)

    grad_gain = jnp.sum(grad_norm * scaled, axis=0)
    weighted = grad_norm * gain
    grad_hidden = (
        grad_out
        + inv_rms * weighted
        - scaled * inv_rms * inv_rms * jnp.mean(weighted * hidden, axis=-1, keepdims=True)
    )
    grad_mix = low(grad_hidden)
    grad_conv_out = product_nt(grad_mix, out_w)
    grad_out_w = low(product_tn(conv_low, grad_mix))
    grad_c = grad_conv_out * convolved
    grad_conv = grad_conv_out * c_branch
    grad_mixed, grad_taps = conv_backward(grad_conv, mixed, taps, matches)
    grad_proj = low(jnp.concatenate([grad_mixed * x_branch, grad_c, grad_mixed * b_branch], axis=1))
    input_grad = grad_hidden + product_nt(grad_proj, in_w)
    grad_in = low(product_tn(tokens, grad_proj))

    down_sum = reduce_plane(grad_down.reshape(chips, 2 * down_rows, width), z, x, core)
    total_down = reduce_ring(down_sum.reshape(2, down_rows, width), y)

    other_rows = lax.dynamic_index_in_dim(grad_unit, 1 - y, 1, keepdims=False)
    own_rows = lax.dynamic_index_in_dim(grad_unit, y, 1, keepdims=False)
    from_gate = ring_shift(other_rows[:, :, :half], 1)
    from_up = ring_shift(other_rows[:, :, half:], 3)
    unit_rows = jnp.concatenate(
        [
            low(wide(own_rows[:, :, :half]) + wide(from_gate)),
            low(wide(own_rows[:, :, half:]) + wide(from_up)),
        ],
        axis=2,
    )
    unit_sum = reduce_plane(unit_rows, z, x, core).reshape(2, rows, 2 * half)
    own = lax.dynamic_index_in_dim(unit_sum, core, 0, keepdims=False)
    other = lax.dynamic_index_in_dim(unit_sum, 1 - core, 0, keepdims=False)
    own_units = wide(own) + wide(ring_shift(own, 2))
    other_units = wide(ring_shift(other, 0, 1)) + wide(ring_shift(other, 2, 1))
    unit_zero = jnp.where(core == 0, own_units, other_units)
    unit_one = jnp.where(core == 0, other_units, own_units)

    def merge(first, second):
        pair = [part.reshape(rows, -1, down_rows) for part in (first, second)]
        return jnp.stack(pair, axis=2).reshape(rows, hidden_units)

    total_gate = merge(unit_zero[:, :half], unit_one[:, :half])
    total_up = merge(unit_zero[:, half:], unit_one[:, half:])

    grad_small = jnp.stack(grad_taps + [grad_gain], axis=1)
    grad_small = jnp.pad(low(grad_small), ((0, 0), (0, AUX - tap_count - 1)))
    mix_blocks = [
        part.reshape(chips, 2, 2, rows, -1) for part in (grad_in, grad_out_w, grad_small)
    ]

    def of_core(which):
        picked = [lax.dynamic_index_in_dim(part, which, 2, keepdims=False) for part in mix_blocks]
        return jnp.concatenate(picked, axis=-1).reshape(chips, 2 * rows, mix_columns)

    mix_rows = low(wide(of_core(core)) + wide(core_swap(of_core(1 - core))))
    mix_sum = reduce_plane(mix_rows, z, x, core)
    total_mix = reduce_ring(mix_sum.reshape(2, rows, mix_columns), y)
    total_small = total_mix[:, in_columns + width :]
    gradients = (
        total_mix[:, :in_columns],
        total_small[:, :tap_count],
        total_mix[:, in_columns : in_columns + width],
        total_small[:, tap_count],
        total_gate,
        total_up,
        total_down,
    )
    bias_one = 1.0 - BETA_ONE**STEP
    bias_two = 1.0 - BETA_TWO**STEP
    updated = []
    firsts = []
    seconds = []
    for master, moment, variance, gradient, step_rate, decay_rate in zip(
        masters, moments, squares, gradients, STEP_RATES, DECAY_RATES
    ):
        first_new = BETA_ONE * moment + (1.0 - BETA_ONE) * gradient
        second_new = BETA_TWO * variance + (1.0 - BETA_TWO) * gradient * gradient
        normalized = first_new / bias_one / (jnp.sqrt(second_new / bias_two) + ADAM_EPS)
        updated.append(master - step_rate * (normalized + decay_rate * master))
        firsts.append(first_new)
        seconds.append(second_new)
    return (block_out, input_grad, *updated, *firsts, *seconds)


def solution(mesh):
    grid = Mesh(mesh.devices.reshape(2, SIDE, SIDE, 2, 2), AXES)
    by_token = P(AXES, None)
    matrix, vector = P(SHARD, None), P(SHARD)
    group = (matrix, matrix, matrix, vector, matrix, matrix, matrix)
    return jax.shard_map(
        body,
        mesh=grid,
        in_specs=(by_token, by_token, P(), P(), *group, *group, *group),
        out_specs=(by_token, by_token, *group, *group, *group),
        check_vma=False,
    )
```

```python
import jax
import jax.numpy as jnp
from jax import lax
from jax.experimental import pallas as pl
from jax.experimental.pallas import tpu as pltpu
from jax.sharding import Mesh
from jax.sharding import PartitionSpec as P

STEP = 10
NORM_EPS = 1e-05
BETA_ONE = 0.9
BETA_TWO = 0.95
ADAM_EPS = 1e-08
STEP_RATES = (0.02, 0.3, 0.02, 0.3, 0.02, 0.02, 0.02)
DECAY_RATES = (0.1, 0.0, 0.1, 0.0, 0.1, 0.1, 0.1)

AXES = ("rep", "z", "x", "y", "core")
SHARD = ("z", "x", "y", "core")
SIDE = 4
AUX = 128


def layout(seq_lengths, seq_device, device, row_count):
    owned_len = jnp.where(seq_device == device, seq_lengths, 0)
    seq_ends = jnp.cumsum(owned_len, dtype=jnp.int32)
    slot_index = jnp.arange(row_count, dtype=jnp.int32)
    segment = jnp.sum(
        (seq_ends[None, :] <= slot_index[:, None]).astype(jnp.int32), axis=1, dtype=jnp.int32
    )
    live_rows = (slot_index < seq_ends[-1]).astype(jnp.int32)
    return (segment, live_rows)


def product(left, right):
    return jnp.dot(left, right, preferred_element_type=jnp.float32)


def product_nt(left, right):
    return lax.dot_general(
        left, right, (((1,), (1,)), ((), ())), preferred_element_type=jnp.float32
    )


def product_tn(left, right):
    return lax.dot_general(
        left, right, (((0,), (0,)), ((), ())), preferred_element_type=jnp.float32
    )


def conv_forward(mixed, taps, segment):
    summed = mixed * taps[0]
    matches = []
    for offset in range(1, len(taps)):
        earlier = jnp.pad(mixed, ((offset, 0), (0, 0)))[:-offset]
        same_seq = (jnp.pad(segment, (offset, 0), constant_values=-1)[:-offset] == segment)[:, None]
        matches.append(same_seq)
        summed = summed + jnp.where(same_seq, earlier * taps[offset], 0.0)
    return (summed, matches)


def conv_backward(gradient, mixed, taps, matches):
    grad_mixed = gradient * taps[0]
    grad_taps = [jnp.sum(gradient * mixed, axis=0)]
    for offset in range(1, len(taps)):
        masked = jnp.where(matches[offset - 1], gradient, 0.0)
        later = jnp.pad(masked, ((0, offset), (0, 0)))[offset:]
        grad_mixed = grad_mixed + later * taps[offset]
        earlier = jnp.pad(mixed, ((offset, 0), (0, 0)))[:-offset]
        grad_taps.append(jnp.sum(masked * earlier, axis=0))
    return (grad_mixed, grad_taps)


def low(value):
    return value.astype(jnp.bfloat16)


def wide(value):
    return value.astype(jnp.float32)


def after(value, *earlier):
    return lax.optimization_barrier((value,) + earlier)[0]


def plane_shift(value, distance, turn):
    pairs = []
    for z in range(SIDE):
        for x in range(SIDE):
            for core in range(2):
                if (core + turn) % 2 == 0:
                    to_z, to_x = z, (x + distance) % SIDE
                else:
                    to_z, to_x = (z + distance) % SIDE, x
                pairs.append(((z * SIDE + x) * 2 + core, (to_z * SIDE + to_x) * 2 + core))
    return lax.ppermute(value, ("z", "x", "core"), pairs)


def ring_shift(value, distance, swap=0):
    pairs = []
    for y in range(SIDE):
        for core in range(2):
            pairs.append((y * 2 + core, (y + distance) % SIDE * 2 + (core + swap) % 2))
    return lax.ppermute(value, ("rep", "y", "core"), pairs)


def core_swap(value):
    return lax.ppermute(value, "core", [(0, 1), (1, 0)])


def pair_swap(value):
    return lax.ppermute(value, "y", [(0, 1), (1, 0)])


def in_order(index, mine, other):
    first = jnp.where(index == 0, mine, other)
    second = jnp.where(index == 0, other, mine)
    return jnp.concatenate([first, second], axis=0)


def turn_spec(block, turn):
    lead = block[0]

    def where(d, k, index):
        at = jnp.where(d == turn, k, jnp.where(d < turn, 0, SIDE - 1))
        return (at,) + (0,) * (len(block) - 1)

    assert lead == 1
    return pl.BlockSpec(block, where)


def spread_blocks(sources, index, out_shapes, out_specs, columns):
    count = len(sources)

    def kernel(index_ref, *refs):
        ins, outs = refs[:count], refs[count:]
        for d in range(count):

            @pl.when(pl.program_id(0) == d)
            def _(source=ins[d]):
                for out, (start, size) in zip(outs, columns):
                    out[...] = source[..., pl.ds(start, size)].reshape(out.shape)

    moved = 2 * sum(source.size * source.dtype.itemsize for source in sources)
    return pl.pallas_call(
        kernel,
        out_shape=out_shapes,
        grid_spec=pltpu.PrefetchScalarGridSpec(
            num_scalar_prefetch=1,
            grid=(count, SIDE),
            in_specs=[turn_spec((1,) + s.shape[1:], d) for d, s in enumerate(sources)],
            out_specs=out_specs,
        ),
        compiler_params=pltpu.CompilerParams(vmem_limit_bytes=48 * 1024 * 1024),
        cost_estimate=pl.CostEstimate(flops=0, bytes_accessed=moved, transcendentals=0),
    )(index, *sources)


def pick_blocks(source, index):
    block = (1,) + source.shape[1:]

    def kernel(index_ref, block_ref, *outs):
        for d in range(SIDE):

            @pl.when(pl.program_id(0) == d)
            def _(out=outs[d]):
                out[...] = block_ref[...]

    moved = 2 * source.size * source.dtype.itemsize
    shape = jax.ShapeDtypeStruct((SIDE,) + source.shape[1:], source.dtype)
    rest = (0,) * (source.ndim - 1)
    return pl.pallas_call(
        kernel,
        out_shape=[shape] * SIDE,
        grid_spec=pltpu.PrefetchScalarGridSpec(
            num_scalar_prefetch=1,
            grid=(SIDE, SIDE),
            in_specs=[pl.BlockSpec(block, lambda d, k, index: (index[d * SIDE + k],) + rest)],
            out_specs=[turn_spec(block, d) for d in range(SIDE)],
        ),
        compiler_params=pltpu.CompilerParams(vmem_limit_bytes=48 * 1024 * 1024),
        cost_estimate=pl.CostEstimate(flops=0, bytes_accessed=moved, transcendentals=0),
    )(index, source)


def gather_plane(block):
    first = [block] + [plane_shift(block, d, 0) for d in (1, 2, 3)]
    joined = jnp.concatenate(first, axis=0)
    return [joined] + [plane_shift(joined, d, 1) for d in (1, 2, 3)]


def plane_places(z, x, core):
    places = []
    for d2 in range(SIDE):
        for d1 in range(SIDE):
            at_z = jnp.where(core == 0, (z - d2) % SIDE, (z - d1) % SIDE)
            at_x = jnp.where(core == 0, (x - d1) % SIDE, (x - d2) % SIDE)
            places.append(at_z * SIDE + at_x)
    return jnp.stack(places).astype(jnp.int32)


def plane_sources(z, x, core):
    picks = []
    for d in range(SIDE):
        for k in range(SIDE):
            at_z = jnp.where(core == 0, (z + d) % SIDE, k)
            at_x = jnp.where(core == 0, k, (x + d) % SIDE)
            picks.append(at_z * SIDE + at_x)
    return jnp.stack(picks).astype(jnp.int32)


def sum_wide(parts):
    total = wide(parts[0])
    for part in parts[1:]:
        total = total + wide(part)
    return total


def reduce_plane(blocks, z, x, core):
    messages = pick_blocks(blocks, plane_sources(z, x, core))
    parts = [messages[0]] + [plane_shift(messages[d], d, 1) for d in (1, 2, 3)]
    summed = low(sum_wide(parts))
    me = jnp.where(core == 0, x, z)
    pick = lambda d: lax.dynamic_index_in_dim(summed, (me + d) % SIDE, 0, keepdims=False)
    return low(sum_wide([pick(0)] + [plane_shift(pick(d), d, 0) for d in (1, 2, 3)]))


def reduce_ring(pair, y):
    own = lax.dynamic_index_in_dim(pair, y, 0, keepdims=False)
    other = lax.dynamic_index_in_dim(pair, 1 - y, 0, keepdims=False)
    return sum_wide([own, ring_shift(other, 1), ring_shift(other, 3), ring_shift(own, 2)])


def body(
    tokens,
    cotangent,
    seq_lengths,
    seq_device,
    in_weight,
    conv_kernel,
    out_weight,
    norm_gain,
    gate_weight,
    up_weight,
    down_weight,
    moment_in,
    moment_conv,
    moment_out,
    moment_gain,
    moment_gate,
    moment_up,
    moment_down,
    square_in,
    square_conv,
    square_out,
    square_gain,
    square_gate,
    square_up,
    square_down,
):
    masters = (in_weight, conv_kernel, out_weight, norm_gain, gate_weight, up_weight, down_weight)
    moments = (moment_in, moment_conv, moment_out, moment_gain, moment_gate, moment_up, moment_down)
    squares = (square_in, square_conv, square_out, square_gain, square_gate, square_up, square_down)
    rep, z, x, y, core = [lax.axis_index(name) for name in AXES]
    device = (((rep * SIDE + z) * SIDE + x) * 2 + y) * 2 + core
    slots, width = tokens.shape
    rows = in_weight.shape[0]
    hidden_units = gate_weight.shape[1]
    half = hidden_units // 2
    down_rows = down_weight.shape[0]
    chips = SIDE * SIDE
    tap_count = conv_kernel.shape[1]
    in_columns = in_weight.shape[1]
    mix_columns = in_columns + width + AUX

    segment, live_rows = layout(seq_lengths, seq_device, device, slots)
    live_float = wide(live_rows)[:, None]
    places = plane_places(z, x, core)

    small = jnp.concatenate([conv_kernel, norm_gain[:, None]], axis=1)
    small = jnp.pad(low(small), ((0, 0), (0, AUX - tap_count - 1)))
    mix_local = jnp.concatenate([low(in_weight), low(out_weight), small], axis=1)
    mix_pair = in_order(y, mix_local, pair_swap(mix_local))
    mix_first = [mix_pair] + [plane_shift(mix_pair, d, 0) for d in (1, 2, 3)]
    mix_joined = jnp.concatenate(mix_first, axis=0)
    mix_own = [mix_joined] + [plane_shift(mix_joined, d, 1) for d in (1, 2, 3)]
    mix_other = [core_swap(part) for part in mix_own]
    other_places = plane_places(z, x, 1 - core)
    parts = [part.reshape(SIDE, 2, rows, mix_columns) for part in mix_own + mix_other]

    both = jnp.stack([core, 1 - core]).astype(jnp.int32)
    mix_index = jnp.concatenate([places, other_places, both])

    def mix_place(d, k, index):
        return (index[d * SIDE + k], 0, index[2 * chips + d // SIDE], 0, 0)

    mix_bounds = [(0, in_columns), (in_columns, width), (in_columns + width, AUX)]
    in_w, out_w, small_w = spread_blocks(
        parts,
        mix_index,
        [
            jax.ShapeDtypeStruct((chips, 2, 2, rows, columns), jnp.bfloat16)
            for _, columns in mix_bounds
        ],
        [pl.BlockSpec((1, 2, 1, rows, columns), mix_place) for _, columns in mix_bounds],
        mix_bounds,
    )
    in_w = in_w.reshape(width, in_columns)
    out_w = out_w.reshape(width, width)
    small_w = wide(small_w.reshape(width, AUX)[:, : tap_count + 1]).T
    taps = [small_w[k] for k in range(tap_count)]
    gain = small_w[tap_count]

    def by_core(weight):
        return low(weight).reshape(rows, -1, 2, down_rows)

    gate_split, up_split = by_core(gate_weight), by_core(up_weight)
    unit_halves = [
        jnp.concatenate(
            [gate_split[:, :, c].reshape(rows, half), up_split[:, :, c].reshape(rows, half)], axis=1
        )
        for c in range(2)
    ]
    mine = jnp.where(core == 0, unit_halves[0], unit_halves[1])
    theirs = jnp.where(core == 0, unit_halves[1], unit_halves[0])
    unit_pair = in_order(core, mine, core_swap(theirs))
    unit_pair = after(unit_pair, *mix_first)
    unit_first = [unit_pair] + [plane_shift(unit_pair, d, 0) for d in (1, 2, 3)]
    unit_joined = after(jnp.concatenate(unit_first, axis=0), *mix_own)
    unit_own = [unit_joined] + [plane_shift(unit_joined, d, 1) for d in (1, 2, 3)]
    unit_other = [ring_shift(part, 1 if i < 2 else 3) for i, part in enumerate(unit_own)]
    parts = [part.reshape(SIDE, 2 * rows, 2 * half) for part in unit_own + unit_other]

    unit_index = jnp.concatenate([places, jnp.stack([y, 1 - y]).astype(jnp.int32)])

    def unit_place(d, k, index):
        return (index[d % SIDE * SIDE + k], index[chips + d // SIDE], 0, 0)

    (unit_w,) = spread_blocks(
        parts,
        unit_index,
        [jax.ShapeDtypeStruct((chips, 2, 2 * rows, 2 * half), jnp.bfloat16)],
        [pl.BlockSpec((1, 1, 2 * rows, 2 * half), unit_place)],
        [(0, 2 * half)],
    )
    unit_w = unit_w.reshape(width, 2 * half)

    down_low = low(down_weight)
    down_pair = in_order(y, down_low, pair_swap(down_low))
    down_pair = after(down_pair, *unit_first)
    down_first = [down_pair] + [plane_shift(down_pair, d, 0) for d in (1, 2, 3)]
    down_joined = after(jnp.concatenate(down_first, axis=0), *unit_own)
    down_own = [down_joined] + [plane_shift(down_joined, d, 1) for d in (1, 2, 3)]
    parts = [part.reshape(SIDE, 2 * down_rows, width) for part in down_own]

    (down_w,) = spread_blocks(
        parts,
        places,
        [jax.ShapeDtypeStruct((chips, 2 * down_rows, width), jnp.bfloat16)],
        [pl.BlockSpec((1, 2 * down_rows, width), lambda d, k, index: (index[d * SIDE + k], 0, 0))],
        [(0, width)],
    )
    down_w = down_w.reshape(half, width)

    projected = product(tokens, in_w)
    b_branch = projected[:, :width]
    c_branch = projected[:, width : 2 * width]
    x_branch = projected[:, 2 * width :]
    mixed = b_branch * x_branch
    convolved, matches = conv_forward(mixed, taps, segment)
    conv_low = low(c_branch * convolved)
    hidden = wide(tokens) + product(conv_low, out_w)
    inv_rms = lax.rsqrt(jnp.mean(hidden * hidden, axis=-1, keepdims=True) + NORM_EPS)
    scaled = hidden * inv_rms
    normed = low(scaled * gain)

    grad_out = wide(cotangent) * live_float
    grad_low = low(grad_out)
    grad_both = jnp.concatenate([grad_low, core_swap(grad_low)], axis=0)
    normed_both = jnp.concatenate([normed, core_swap(normed)], axis=0)
    pre = product(normed_both, unit_w)
    gate_pre, up_pre = pre[:, :half], pre[:, half:]
    sigmoid_gate = jax.nn.sigmoid(gate_pre)
    silu_gate = gate_pre * sigmoid_gate
    act_low = low(silu_gate * up_pre)
    ffn_part = product(act_low, down_w)
    grad_act = product_nt(grad_both, down_w)
    grad_down = low(product_tn(act_low, grad_both))
    grad_up = low(grad_act * silu_gate)
    grad_gate = low(grad_act * up_pre * sigmoid_gate * (1.0 + gate_pre * (1.0 - sigmoid_gate)))
    grad_pre = jnp.concatenate([grad_gate, grad_up], axis=1)
    norm_part = product_nt(grad_pre, unit_w)
    grad_norm = norm_part[:slots] + wide(core_swap(low(norm_part[slots:])))
    ffn_out = ffn_part[:slots] + wide(core_swap(low(ffn_part[slots:])))
    block_out = low((hidden + ffn_out) * live_float)
    grad_unit = low(product_tn(normed_both, grad_pre)).reshape(chips, 2, 2 * rows, 2 * half)

    grad_gain = jnp.sum(grad_norm * scaled, axis=0)
    weighted = grad_norm * gain
    grad_hidden = (
        grad_out
        + inv_rms * weighted
        - scaled * inv_rms * inv_rms * jnp.mean(weighted * hidden, axis=-1, keepdims=True)
    )
    grad_mix = low(grad_hidden)
    grad_conv_out = product_nt(grad_mix, out_w)
    grad_out_w = low(product_tn(conv_low, grad_mix))
    grad_c = grad_conv_out * convolved
    grad_conv = grad_conv_out * c_branch
    grad_mixed, grad_taps = conv_backward(grad_conv, mixed, taps, matches)
    grad_proj = low(jnp.concatenate([grad_mixed * x_branch, grad_c, grad_mixed * b_branch], axis=1))
    input_grad = grad_hidden + product_nt(grad_proj, in_w)
    grad_in = low(product_tn(tokens, grad_proj))

    down_sum = reduce_plane(grad_down.reshape(chips, 2 * down_rows, width), z, x, core)
    total_down = reduce_ring(down_sum.reshape(2, down_rows, width), y)

    other_rows = lax.dynamic_index_in_dim(grad_unit, 1 - y, 1, keepdims=False)
    own_rows = lax.dynamic_index_in_dim(grad_unit, y, 1, keepdims=False)
    from_gate = ring_shift(other_rows[:, :, :half], 1)
    from_up = ring_shift(other_rows[:, :, half:], 3)
    unit_rows = jnp.concatenate(
        [
            low(wide(own_rows[:, :, :half]) + wide(from_gate)),
            low(wide(own_rows[:, :, half:]) + wide(from_up)),
        ],
        axis=2,
    )
    unit_sum = reduce_plane(unit_rows, z, x, core).reshape(2, rows, 2 * half)
    own = lax.dynamic_index_in_dim(unit_sum, core, 0, keepdims=False)
    other = lax.dynamic_index_in_dim(unit_sum, 1 - core, 0, keepdims=False)
    own_units = wide(own) + wide(ring_shift(own, 2))
    other_units = wide(ring_shift(other, 0, 1)) + wide(ring_shift(other, 2, 1))
    unit_zero = jnp.where(core == 0, own_units, other_units)
    unit_one = jnp.where(core == 0, other_units, own_units)

    def merge(first, second):
        pair = [part.reshape(rows, -1, down_rows) for part in (first, second)]
        return jnp.stack(pair, axis=2).reshape(rows, hidden_units)

    total_gate = merge(unit_zero[:, :half], unit_one[:, :half])
    total_up = merge(unit_zero[:, half:], unit_one[:, half:])

    grad_small = jnp.stack(grad_taps + [grad_gain], axis=1)
    grad_small = jnp.pad(low(grad_small), ((0, 0), (0, AUX - tap_count - 1)))
    mix_blocks = [
        part.reshape(chips, 2, 2, rows, -1) for part in (grad_in, grad_out_w, grad_small)
    ]

    def of_core(which):
        picked = [lax.dynamic_index_in_dim(part, which, 2, keepdims=False) for part in mix_blocks]
        return jnp.concatenate(picked, axis=-1).reshape(chips, 2 * rows, mix_columns)

    mix_rows = low(wide(of_core(core)) + wide(core_swap(of_core(1 - core))))
    mix_sum = reduce_plane(mix_rows, z, x, core)
    total_mix = reduce_ring(mix_sum.reshape(2, rows, mix_columns), y)
    total_small = total_mix[:, in_columns + width :]
    gradients = (
        total_mix[:, :in_columns],
        total_small[:, :tap_count],
        total_mix[:, in_columns : in_columns + width],
        total_small[:, tap_count],
        total_gate,
        total_up,
        total_down,
    )
    bias_one = 1.0 - BETA_ONE**STEP
    bias_two = 1.0 - BETA_TWO**STEP
    updated = []
    firsts = []
    seconds = []
    for master, moment, variance, gradient, step_rate, decay_rate in zip(
        masters, moments, squares, gradients, STEP_RATES, DECAY_RATES
    ):
        first_new = BETA_ONE * moment + (1.0 - BETA_ONE) * gradient
        second_new = BETA_TWO * variance + (1.0 - BETA_TWO) * gradient * gradient
        normalized = first_new / bias_one / (jnp.sqrt(second_new / bias_two) + ADAM_EPS)
        updated.append(master - step_rate * (normalized + decay_rate * master))
        firsts.append(first_new)
        seconds.append(second_new)
    return (block_out, input_grad, *updated, *firsts, *seconds)


def solution(mesh):
    grid = Mesh(mesh.devices.reshape(2, SIDE, SIDE, 2, 2), AXES)
    by_token = P(AXES, None)
    matrix, vector = P(SHARD, None), P(SHARD)
    group = (matrix, matrix, matrix, vector, matrix, matrix, matrix)
    return jax.shard_map(
        body,
        mesh=grid,
        in_specs=(by_token, by_token, P(), P(), *group, *group, *group),
        out_specs=(by_token, by_token, *group, *group, *group),
        check_vma=False,
    )
```

```python
import jax
import jax.numpy as jnp
from jax import lax
from jax.experimental import pallas as pl
from jax.experimental.pallas import tpu as pltpu
from jax.sharding import Mesh
from jax.sharding import PartitionSpec as P

STEP = 10
NORM_EPS = 1e-05
BETA_ONE = 0.9
BETA_TWO = 0.95
ADAM_EPS = 1e-08
STEP_RATES = (0.02, 0.3, 0.02, 0.3, 0.02, 0.02, 0.02)
DECAY_RATES = (0.1, 0.0, 0.1, 0.0, 0.1, 0.1, 0.1)

AXES = ("rep", "z", "x", "y", "core")
SHARD = ("z", "x", "y", "core")
SIDE = 4
AUX = 128


def layout(seq_lengths, seq_device, device, row_count):
    owned_len = jnp.where(seq_device == device, seq_lengths, 0)
    seq_ends = jnp.cumsum(owned_len, dtype=jnp.int32)
    slot_index = jnp.arange(row_count, dtype=jnp.int32)
    segment = jnp.sum(
        (seq_ends[None, :] <= slot_index[:, None]).astype(jnp.int32), axis=1, dtype=jnp.int32
    )
    live_rows = (slot_index < seq_ends[-1]).astype(jnp.int32)
    return (segment, live_rows)


def product(left, right):
    return jnp.dot(left, right, preferred_element_type=jnp.float32)


def product_nt(left, right):
    return lax.dot_general(
        left, right, (((1,), (1,)), ((), ())), preferred_element_type=jnp.float32
    )


def product_tn(left, right):
    return lax.dot_general(
        left, right, (((0,), (0,)), ((), ())), preferred_element_type=jnp.float32
    )


def conv_forward(mixed, taps, segment):
    summed = mixed * taps[0]
    matches = []
    for offset in range(1, len(taps)):
        earlier = jnp.pad(mixed, ((offset, 0), (0, 0)))[:-offset]
        same_seq = (jnp.pad(segment, (offset, 0), constant_values=-1)[:-offset] == segment)[:, None]
        matches.append(same_seq)
        summed = summed + jnp.where(same_seq, earlier * taps[offset], 0.0)
    return (summed, matches)


def conv_backward(gradient, mixed, taps, matches):
    grad_mixed = gradient * taps[0]
    grad_taps = [jnp.sum(gradient * mixed, axis=0)]
    for offset in range(1, len(taps)):
        masked = jnp.where(matches[offset - 1], gradient, 0.0)
        later = jnp.pad(masked, ((0, offset), (0, 0)))[offset:]
        grad_mixed = grad_mixed + later * taps[offset]
        earlier = jnp.pad(mixed, ((offset, 0), (0, 0)))[:-offset]
        grad_taps.append(jnp.sum(masked * earlier, axis=0))
    return (grad_mixed, grad_taps)


def low(value):
    return value.astype(jnp.bfloat16)


def wide(value):
    return value.astype(jnp.float32)


def after(value, *earlier):
    return lax.optimization_barrier((value,) + earlier)[0]


def plane_shift(value, distance, turn):
    pairs = []
    for z in range(SIDE):
        for x in range(SIDE):
            for core in range(2):
                if (core + turn) % 2 == 0:
                    to_z, to_x = z, (x + distance) % SIDE
                else:
                    to_z, to_x = (z + distance) % SIDE, x
                pairs.append(((z * SIDE + x) * 2 + core, (to_z * SIDE + to_x) * 2 + core))
    return lax.ppermute(value, ("z", "x", "core"), pairs)


def ring_shift(value, distance, swap=0):
    pairs = []
    for y in range(SIDE):
        for core in range(2):
            pairs.append((y * 2 + core, (y + distance) % SIDE * 2 + (core + swap) % 2))
    return lax.ppermute(value, ("rep", "y", "core"), pairs)


def core_swap(value):
    return lax.ppermute(value, "core", [(0, 1), (1, 0)])


def pair_swap(value):
    return lax.ppermute(value, "y", [(0, 1), (1, 0)])


def diagonal_swap(value):
    return lax.ppermute(value, ("y", "core"), [(0, 3), (1, 2), (2, 1), (3, 0)])


def in_order(index, mine, other):
    first = jnp.where(index == 0, mine, other)
    second = jnp.where(index == 0, other, mine)
    return jnp.concatenate([first, second], axis=0)


def copy_kernel(loads, stores):
    def kernel(index_ref, *refs):
        load_sems, store_sems = refs[-2:]
        fills = [
            pltpu.make_async_copy(source, target, load_sems.at[i])
            for i, (source, target) in enumerate(loads(index_ref, refs))
        ]
        for fill in fills:
            fill.start()
        empties = []
        for i, (needs, source, target) in enumerate(stores(index_ref, refs)):
            for need in needs:
                fills[need].wait()
            empties.append(pltpu.make_async_copy(source, target, store_sems.at[i]))
            empties[-1].start()
        for empty in empties:
            empty.wait()

    return kernel


def copy_call(kernel, index, sources, out_shapes, scratch, load_count, store_count):
    moved = 2 * sum(source.size * source.dtype.itemsize for source in sources)
    return pl.pallas_call(
        kernel,
        out_shape=out_shapes,
        in_specs=[pl.BlockSpec(memory_space=pltpu.SMEM)]
        + [pl.BlockSpec(memory_space=pl.ANY)] * len(sources),
        out_specs=[pl.BlockSpec(memory_space=pl.ANY)] * len(out_shapes),
        scratch_shapes=scratch
        + [pltpu.SemaphoreType.DMA((load_count,)), pltpu.SemaphoreType.DMA((store_count,))],
        compiler_params=pltpu.CompilerParams(vmem_limit_bytes=40 * 1024 * 1024),
        cost_estimate=pl.CostEstimate(flops=0, bytes_accessed=moved, transcendentals=0),
    )(index, *sources)


def spread_blocks(sources, index, out_shape, place):
    count = len(sources)

    def loads(index_ref, refs):
        return [(refs[d], refs[count + 1].at[d]) for d in range(count)]

    def stores(index_ref, refs):
        moves = []
        for d in range(count):
            for k in range(SIDE):
                needs = [d] if k == 0 else []
                target = refs[count].at[place(d, k, index_ref)]
                moves.append((needs, refs[count + 1].at[d, k], target))
        return moves

    scratch = [pltpu.VMEM((count,) + sources[0].shape, sources[0].dtype)]
    (out,) = copy_call(
        copy_kernel(loads, stores), index, sources, [out_shape], scratch, count, count * SIDE
    )
    return out


def pick_blocks(source, index):
    shape = (SIDE,) + source.shape[1:]

    def loads(index_ref, refs):
        return [
            (refs[0].at[index_ref[d * SIDE + k]], refs[1 + SIDE].at[d, k])
            for d in range(SIDE)
            for k in range(SIDE)
        ]

    def stores(index_ref, refs):
        return [
            (range(d * SIDE, (d + 1) * SIDE), refs[1 + SIDE].at[d], refs[1 + d])
            for d in range(SIDE)
        ]

    return copy_call(
        copy_kernel(loads, stores),
        index,
        [source],
        [jax.ShapeDtypeStruct(shape, source.dtype)] * SIDE,
        [pltpu.VMEM((SIDE,) + shape, source.dtype)],
        SIDE * SIDE,
        SIDE,
    )


def plane_places(z, x, core):
    places = []
    for d2 in range(SIDE):
        for d1 in range(SIDE):
            at_z = jnp.where(core == 0, (z - d2) % SIDE, (z - d1) % SIDE)
            at_x = jnp.where(core == 0, (x - d1) % SIDE, (x - d2) % SIDE)
            places.append(at_z * SIDE + at_x)
    return jnp.stack(places).astype(jnp.int32)


def plane_sources(z, x, core):
    picks = []
    for d in range(SIDE):
        for k in range(SIDE):
            at_z = jnp.where(core == 0, (z + d) % SIDE, k)
            at_x = jnp.where(core == 0, k, (x + d) % SIDE)
            picks.append(at_z * SIDE + at_x)
    return jnp.stack(picks).astype(jnp.int32)


def sum_wide(parts):
    total = wide(parts[0])
    for part in parts[1:]:
        total = total + wide(part)
    return total


def plane_first(messages):
    return [messages[0]] + [plane_shift(messages[d], d, 1) for d in (1, 2, 3)]


def plane_second(parts, z, x, core):
    summed = low(sum_wide(parts))
    me = jnp.where(core == 0, x, z)
    pick = lambda d: lax.dynamic_index_in_dim(summed, (me + d) % SIDE, 0, keepdims=False)
    return [pick(0)] + [plane_shift(pick(d), d, 0) for d in (1, 2, 3)]


def ring_parts(pair, y):
    own = lax.dynamic_index_in_dim(pair, y, 0, keepdims=False)
    other = lax.dynamic_index_in_dim(pair, 1 - y, 0, keepdims=False)
    return [own, ring_shift(other, 1), ring_shift(other, 3), ring_shift(own, 2)]


def body(
    tokens,
    cotangent,
    seq_lengths,
    seq_device,
    in_weight,
    conv_kernel,
    out_weight,
    norm_gain,
    gate_weight,
    up_weight,
    down_weight,
    moment_in,
    moment_conv,
    moment_out,
    moment_gain,
    moment_gate,
    moment_up,
    moment_down,
    square_in,
    square_conv,
    square_out,
    square_gain,
    square_gate,
    square_up,
    square_down,
):
    masters = (in_weight, conv_kernel, out_weight, norm_gain, gate_weight, up_weight, down_weight)
    moments = (moment_in, moment_conv, moment_out, moment_gain, moment_gate, moment_up, moment_down)
    squares = (square_in, square_conv, square_out, square_gain, square_gate, square_up, square_down)
    rep, z, x, y, core = [lax.axis_index(name) for name in AXES]
    device = (((rep * SIDE + z) * SIDE + x) * 2 + y) * 2 + core
    slots, width = tokens.shape
    rows = in_weight.shape[0]
    hidden_units = gate_weight.shape[1]
    half = hidden_units // 2
    down_rows = down_weight.shape[0]
    chips = SIDE * SIDE
    tap_count = conv_kernel.shape[1]
    in_columns = in_weight.shape[1]
    mix_columns = in_columns + width + AUX

    segment, live_rows = layout(seq_lengths, seq_device, device, slots)
    live_float = wide(live_rows)[:, None]
    places = plane_places(z, x, core)

    small = jnp.concatenate([conv_kernel, norm_gain[:, None]], axis=1)
    small = jnp.pad(low(small), ((0, 0), (0, AUX - tap_count - 1)))
    mix_local = jnp.concatenate([low(in_weight), low(out_weight), small], axis=1)
    mix_cores = [mix_local, core_swap(mix_local), pair_swap(mix_local), diagonal_swap(mix_local)]
    mix_chips = in_order(
        y, in_order(core, mix_cores[0], mix_cores[1]), in_order(core, mix_cores[2], mix_cores[3])
    )
    mix_w = lax.all_gather(mix_chips, ("z", "x"), axis=0, tiled=True)
    in_w = mix_w[:, :in_columns]
    out_w = mix_w[:, in_columns : in_columns + width]
    small_w = mix_w[:, in_columns + width :]
    small_w = wide(small_w[:, : tap_count + 1]).T
    taps = [small_w[k] for k in range(tap_count)]
    gain = small_w[tap_count]

    def by_core(weight):
        return low(weight).reshape(rows, -1, 2, down_rows)

    gate_split, up_split = by_core(gate_weight), by_core(up_weight)
    unit_halves = [
        jnp.concatenate(
            [gate_split[:, :, c].reshape(rows, half), up_split[:, :, c].reshape(rows, half)], axis=1
        )
        for c in range(2)
    ]
    mine = jnp.where(core == 0, unit_halves[0], unit_halves[1])
    theirs = jnp.where(core == 0, unit_halves[1], unit_halves[0])
    unit_pair = in_order(core, mine, core_swap(theirs))
    unit_first = [unit_pair] + [plane_shift(unit_pair, d, 0) for d in (1, 2, 3)]
    unit_joined = jnp.concatenate(unit_first, axis=0)
    unit_own = [unit_joined] + [plane_shift(unit_joined, d, 1) for d in (1, 2, 3)]
    unit_other = [ring_shift(part, 1 if i % 2 == 0 else 3) for i, part in enumerate(unit_own)]
    parts = [part.reshape(SIDE, 2 * rows, 2 * half) for part in unit_own + unit_other]

    unit_index = jnp.concatenate([places, jnp.stack([y, 1 - y]).astype(jnp.int32)])

    unit_w = spread_blocks(
        parts,
        unit_index,
        jax.ShapeDtypeStruct((chips, 2, 2 * rows, 2 * half), jnp.bfloat16),
        lambda d, k, index: (index[d % SIDE * SIDE + k], index[chips + d // SIDE]),
    )
    unit_w = unit_w.reshape(width, 2 * half)

    down_low = low(down_weight)
    down_pair = in_order(y, down_low, pair_swap(down_low))
    down_pair = after(down_pair, *unit_first)
    down_first = [down_pair] + [plane_shift(down_pair, d, 0) for d in (1, 2, 3)]
    down_joined = after(jnp.concatenate(down_first, axis=0), *unit_own)
    down_own = [down_joined] + [plane_shift(down_joined, d, 1) for d in (1, 2, 3)]
    parts = [part.reshape(SIDE, 2 * down_rows, width) for part in down_own]

    down_w = spread_blocks(
        parts,
        places,
        jax.ShapeDtypeStruct((chips, 2 * down_rows, width), jnp.bfloat16),
        lambda d, k, index: index[d * SIDE + k],
    )
    down_w = down_w.reshape(half, width)

    projected = product(tokens, in_w)
    b_branch = projected[:, :width]
    c_branch = projected[:, width : 2 * width]
    x_branch = projected[:, 2 * width :]
    mixed = b_branch * x_branch
    convolved, matches = conv_forward(mixed, taps, segment)
    conv_low = low(c_branch * convolved)
    hidden = wide(tokens) + product(conv_low, out_w)
    inv_rms = lax.rsqrt(jnp.mean(hidden * hidden, axis=-1, keepdims=True) + NORM_EPS)
    scaled = hidden * inv_rms
    normed = low(scaled * gain)

    grad_out = wide(cotangent) * live_float
    grad_low = low(grad_out)
    grad_both = jnp.concatenate([grad_low, core_swap(grad_low)], axis=0)
    normed_both = jnp.concatenate([normed, core_swap(normed)], axis=0)
    pre = product(normed_both, unit_w)
    gate_pre, up_pre = pre[:, :half], pre[:, half:]
    sigmoid_gate = jax.nn.sigmoid(gate_pre)
    silu_gate = gate_pre * sigmoid_gate
    act_low = low(silu_gate * up_pre)
    ffn_part = product(act_low, down_w)
    grad_act = product_nt(grad_both, down_w)
    grad_up = low(grad_act * silu_gate)
    grad_gate = low(grad_act * up_pre * sigmoid_gate * (1.0 + gate_pre * (1.0 - sigmoid_gate)))
    sources = plane_sources(z, x, core)

    grad_down = low(product_tn(act_low, grad_both)).reshape(chips, 2 * down_rows, width)
    down_messages = pick_blocks(grad_down, sources)
    down_parts = plane_first(down_messages)

    def over_ring(left, right):
        blocks = low(product_tn(left, right)).reshape(chips, 2, 2 * rows, half)
        other_rows = lax.dynamic_index_in_dim(blocks, 1 - y, 1, keepdims=False)
        own_rows = lax.dynamic_index_in_dim(blocks, y, 1, keepdims=False)
        middle = chips // 2
        halves = [ring_shift(other_rows[:middle], 1), ring_shift(other_rows[middle:], 3)]
        return own_rows, halves

    def join_ring(own_rows, halves):
        return low(wide(own_rows) + wide(jnp.concatenate(halves, axis=0)))

    gate_own, gate_halves = over_ring(after(normed_both, *down_messages), grad_gate)
    norm_part = product_nt(grad_gate, unit_w[:, :half]) + product_nt(grad_up, unit_w[:, half:])
    norm_other = core_swap(low(norm_part[slots:]))
    grad_norm = norm_part[:slots] + wide(norm_other)
    up_own, up_halves = over_ring(after(normed_both, *gate_halves), grad_up)
    ffn_out = ffn_part[:slots] + wide(core_swap(low(ffn_part[slots:])))
    block_out = low((hidden + ffn_out) * live_float)
    gate_parts = plane_first(pick_blocks(join_ring(gate_own, gate_halves), sources))
    up_parts = plane_first(pick_blocks(join_ring(up_own, up_halves), sources))

    grad_gain = jnp.sum(grad_norm * scaled, axis=0)
    weighted = grad_norm * gain
    grad_hidden = (
        grad_out
        + inv_rms * weighted
        - scaled * inv_rms * inv_rms * jnp.mean(weighted * hidden, axis=-1, keepdims=True)
    )
    grad_mix = low(grad_hidden)
    grad_conv_out = product_nt(grad_mix, out_w)
    grad_out_w = low(product_tn(conv_low, grad_mix))
    grad_c = grad_conv_out * convolved
    grad_conv = grad_conv_out * c_branch
    grad_mixed, grad_taps = conv_backward(grad_conv, mixed, taps, matches)
    grad_proj = low(jnp.concatenate([grad_mixed * x_branch, grad_c, grad_mixed * b_branch], axis=1))
    input_grad = grad_hidden + product_nt(grad_proj, in_w)
    grad_in = low(product_tn(tokens, grad_proj))

    grad_small = jnp.stack(grad_taps + [grad_gain], axis=1)
    grad_small = jnp.pad(low(grad_small), ((0, 0), (0, AUX - tap_count - 1)))
    mix_blocks = [
        part.reshape(chips, 2, 2, rows, -1) for part in (grad_in, grad_out_w, grad_small)
    ]

    def of_core(which):
        picked = [lax.dynamic_index_in_dim(part, which, 2, keepdims=False) for part in mix_blocks]
        return jnp.concatenate(picked, axis=-1).reshape(chips, 2 * rows, mix_columns)

    mix_rows = low(wide(of_core(core)) + wide(core_swap(of_core(1 - core))))
    mix_messages = pick_blocks(mix_rows, sources)
    mix_parts = plane_first(mix_messages)

    down_sum = low(sum_wide(plane_second(down_parts, z, x, core)))
    total_down = sum_wide(ring_parts(down_sum.reshape(2, down_rows, width), y))

    unit_parts = [
        after(jnp.concatenate(pair, axis=2), *mix_messages) for pair in zip(gate_parts, up_parts)
    ]
    unit_sum = low(sum_wide(plane_second(unit_parts, z, x, core))).reshape(2, rows, 2 * half)
    own = lax.dynamic_index_in_dim(unit_sum, core, 0, keepdims=False)
    other = lax.dynamic_index_in_dim(unit_sum, 1 - core, 0, keepdims=False)
    own_units = wide(own) + wide(ring_shift(own, 2))
    other_units = wide(ring_shift(other, 0, 1)) + wide(ring_shift(other, 2, 1))
    unit_zero = jnp.where(core == 0, own_units, other_units)
    unit_one = jnp.where(core == 0, other_units, own_units)

    def merge(first, second):
        pair = [part.reshape(rows, -1, down_rows) for part in (first, second)]
        return jnp.stack(pair, axis=2).reshape(rows, hidden_units)

    total_gate = merge(unit_zero[:, :half], unit_one[:, :half])
    total_up = merge(unit_zero[:, half:], unit_one[:, half:])

    mix_sum = low(sum_wide(plane_second(mix_parts, z, x, core)))
    mix_terms = ring_parts(mix_sum.reshape(2, rows, mix_columns), y)

    def mix_total(start, size):
        return sum_wide([lax.slice_in_dim(term, start, start + size, axis=1) for term in mix_terms])

    total_small = mix_total(in_columns + width, AUX)
    lane = lax.broadcasted_iota(jnp.int32, total_small.shape, 1)
    small_columns = [
        jnp.sum(jnp.where(lane == k, total_small, 0.0), axis=1) for k in range(tap_count + 1)
    ]
    gradients = (
        mix_total(0, in_columns),
        jnp.stack(small_columns[:tap_count], axis=1),
        mix_total(in_columns, width),
        small_columns[tap_count],
        total_gate,
        total_up,
        total_down,
    )
    bias_one = 1.0 - BETA_ONE**STEP
    bias_two = 1.0 - BETA_TWO**STEP
    updated = []
    firsts = []
    seconds = []
    for master, moment, variance, gradient, step_rate, decay_rate in zip(
        masters, moments, squares, gradients, STEP_RATES, DECAY_RATES
    ):
        first_new = BETA_ONE * moment + (1.0 - BETA_ONE) * gradient
        second_new = BETA_TWO * variance + (1.0 - BETA_TWO) * gradient * gradient
        normalized = first_new / bias_one / (jnp.sqrt(second_new / bias_two) + ADAM_EPS)
        updated.append(master - step_rate * (normalized + decay_rate * master))
        firsts.append(first_new)
        seconds.append(second_new)
    return (block_out, input_grad, *updated, *firsts, *seconds)


def solution(mesh):
    grid = Mesh(mesh.devices.reshape(2, SIDE, SIDE, 2, 2), AXES)
    by_token = P(AXES, None)
    matrix, vector = P(SHARD, None), P(SHARD)
    group = (matrix, matrix, matrix, vector, matrix, matrix, matrix)
    return jax.shard_map(
        body,
        mesh=grid,
        in_specs=(by_token, by_token, P(), P(), *group, *group, *group),
        out_specs=(by_token, by_token, *group, *group, *group),
        check_vma=False,
    )
```

```python
import jax
import jax.numpy as jnp
from jax import lax
from jax.experimental import pallas as pl
from jax.experimental.pallas import tpu as pltpu
from jax.sharding import Mesh
from jax.sharding import PartitionSpec as P

STEP = 10
NORM_EPS = 1e-05
BETA_ONE = 0.9
BETA_TWO = 0.95
ADAM_EPS = 1e-08
STEP_RATES = (0.02, 0.3, 0.02, 0.3, 0.02, 0.02, 0.02)
DECAY_RATES = (0.1, 0.0, 0.1, 0.0, 0.1, 0.1, 0.1)

AXES = ("rep", "z", "x", "y", "core")
SHARD = ("z", "x", "y", "core")
SIDE = 4
AUX = 128


def layout(seq_lengths, seq_device, device, row_count):
    owned_len = jnp.where(seq_device == device, seq_lengths, 0)
    seq_ends = jnp.cumsum(owned_len, dtype=jnp.int32)
    slot_index = jnp.arange(row_count, dtype=jnp.int32)
    segment = jnp.sum(
        (seq_ends[None, :] <= slot_index[:, None]).astype(jnp.int32), axis=1, dtype=jnp.int32
    )
    live_rows = (slot_index < seq_ends[-1]).astype(jnp.int32)
    return (segment, live_rows)


def product(left, right):
    return jnp.dot(left, right, preferred_element_type=jnp.float32)


def product_nt(left, right):
    return lax.dot_general(
        left, right, (((1,), (1,)), ((), ())), preferred_element_type=jnp.float32
    )


def product_tn(left, right):
    return lax.dot_general(
        left, right, (((0,), (0,)), ((), ())), preferred_element_type=jnp.float32
    )


def conv_forward(mixed, taps, segment):
    summed = mixed * taps[0]
    matches = []
    for offset in range(1, len(taps)):
        earlier = jnp.pad(mixed, ((offset, 0), (0, 0)))[:-offset]
        same_seq = (jnp.pad(segment, (offset, 0), constant_values=-1)[:-offset] == segment)[:, None]
        matches.append(same_seq)
        summed = summed + jnp.where(same_seq, earlier * taps[offset], 0.0)
    return (summed, matches)


def conv_backward(gradient, mixed, taps, matches):
    grad_mixed = gradient * taps[0]
    grad_taps = [jnp.sum(gradient * mixed, axis=0)]
    for offset in range(1, len(taps)):
        masked = jnp.where(matches[offset - 1], gradient, 0.0)
        later = jnp.pad(masked, ((0, offset), (0, 0)))[offset:]
        grad_mixed = grad_mixed + later * taps[offset]
        earlier = jnp.pad(mixed, ((offset, 0), (0, 0)))[:-offset]
        grad_taps.append(jnp.sum(masked * earlier, axis=0))
    return (grad_mixed, grad_taps)


def low(value):
    return value.astype(jnp.bfloat16)


def wide(value):
    return value.astype(jnp.float32)


def after(value, *earlier):
    return lax.optimization_barrier((value,) + earlier)[0]


def plane_shift(value, distance, turn):
    pairs = []
    for z in range(SIDE):
        for x in range(SIDE):
            for core in range(2):
                if (core + turn) % 2 == 0:
                    to_z, to_x = z, (x + distance) % SIDE
                else:
                    to_z, to_x = (z + distance) % SIDE, x
                pairs.append(((z * SIDE + x) * 2 + core, (to_z * SIDE + to_x) * 2 + core))
    return lax.ppermute(value, ("z", "x", "core"), pairs)


def ring_shift(value, distance, swap=0):
    pairs = []
    for y in range(SIDE):
        for core in range(2):
            pairs.append((y * 2 + core, (y + distance) % SIDE * 2 + (core + swap) % 2))
    return lax.ppermute(value, ("rep", "y", "core"), pairs)


def ring_turn(value):
    pairs = []
    for y in range(SIDE):
        for core in range(2):
            pairs.append((y * 2 + core, (y + 1 - 2 * core) % SIDE * 2 + core))
    return lax.ppermute(value, ("rep", "y", "core"), pairs)


def core_swap(value):
    return lax.ppermute(value, "core", [(0, 1), (1, 0)])


def pair_swap(value):
    return lax.ppermute(value, "y", [(0, 1), (1, 0)])


def in_order(index, mine, other):
    first = jnp.where(index == 0, mine, other)
    second = jnp.where(index == 0, other, mine)
    return jnp.concatenate([first, second], axis=0)


def copy_kernel(loads, stores):
    def kernel(index_ref, *refs):
        load_sems, store_sems = refs[-2:]
        fills = [
            pltpu.make_async_copy(source, target, load_sems.at[i])
            for i, (source, target) in enumerate(loads(index_ref, refs))
        ]
        for fill in fills:
            fill.start()
        empties = []
        for i, (needs, source, target) in enumerate(stores(index_ref, refs)):
            for need in needs:
                fills[need].wait()
            empties.append(pltpu.make_async_copy(source, target, store_sems.at[i]))
            empties[-1].start()
        for empty in empties:
            empty.wait()

    return kernel


def copy_call(kernel, index, sources, out_shapes, scratch, load_count, store_count):
    moved = 2 * sum(source.size * source.dtype.itemsize for source in sources)
    return pl.pallas_call(
        kernel,
        out_shape=out_shapes,
        in_specs=[pl.BlockSpec(memory_space=pltpu.SMEM)]
        + [pl.BlockSpec(memory_space=pl.ANY)] * len(sources),
        out_specs=[pl.BlockSpec(memory_space=pl.ANY)] * len(out_shapes),
        scratch_shapes=scratch
        + [pltpu.SemaphoreType.DMA((load_count,)), pltpu.SemaphoreType.DMA((store_count,))],
        compiler_params=pltpu.CompilerParams(vmem_limit_bytes=40 * 1024 * 1024),
        cost_estimate=pl.CostEstimate(flops=0, bytes_accessed=moved, transcendentals=0),
    )(index, *sources)


def spread_blocks(sources, index, out_shape, place):
    count, blocks = len(sources), sources[0].shape[0]

    def loads(index_ref, refs):
        return [(refs[d], refs[count + 1].at[d]) for d in range(count)]

    def stores(index_ref, refs):
        moves = []
        for d in range(count):
            for k in range(blocks):
                needs = [d] if k == 0 else []
                target = refs[count].at[place(d, k, index_ref)]
                moves.append((needs, refs[count + 1].at[d, k], target))
        return moves

    scratch = [pltpu.VMEM((count,) + sources[0].shape, sources[0].dtype)]
    (out,) = copy_call(
        copy_kernel(loads, stores), index, sources, [out_shape], scratch, count, count * blocks
    )
    return out


def pick_blocks(source, index):
    shape = (SIDE,) + source.shape[1:]

    def loads(index_ref, refs):
        return [
            (refs[0].at[index_ref[d * SIDE + k]], refs[1 + SIDE].at[d, k])
            for d in range(SIDE)
            for k in range(SIDE)
        ]

    def stores(index_ref, refs):
        return [
            (range(d * SIDE, (d + 1) * SIDE), refs[1 + SIDE].at[d], refs[1 + d])
            for d in range(SIDE)
        ]

    return copy_call(
        copy_kernel(loads, stores),
        index,
        [source],
        [jax.ShapeDtypeStruct(shape, source.dtype)] * SIDE,
        [pltpu.VMEM((SIDE,) + shape, source.dtype)],
        SIDE * SIDE,
        SIDE,
    )


def plane_places(z, x, core):
    places = []
    for d2 in range(SIDE):
        for d1 in range(SIDE):
            at_z = jnp.where(core == 0, (z - d2) % SIDE, (z - d1) % SIDE)
            at_x = jnp.where(core == 0, (x - d1) % SIDE, (x - d2) % SIDE)
            places.append(at_z * SIDE + at_x)
    return jnp.stack(places).astype(jnp.int32)


def plane_sources(z, x, core):
    picks = []
    for d in range(SIDE):
        for k in range(SIDE):
            at_z = jnp.where(core == 0, (z + d) % SIDE, k)
            at_x = jnp.where(core == 0, k, (x + d) % SIDE)
            picks.append(at_z * SIDE + at_x)
    return jnp.stack(picks).astype(jnp.int32)


def sum_wide(parts):
    total = wide(parts[0])
    for part in parts[1:]:
        total = total + wide(part)
    return total


def plane_first(messages):
    return [messages[0]] + [plane_shift(messages[d], d, 1) for d in (1, 2, 3)]


def plane_second(parts, z, x, core):
    summed = low(sum_wide(parts))
    me = jnp.where(core == 0, x, z)
    pick = lambda d: lax.dynamic_index_in_dim(summed, (me + d) % SIDE, 0, keepdims=False)
    return [pick(0)] + [plane_shift(pick(d), d, 0) for d in (1, 2, 3)]


def ring_parts(pair, y):
    own = lax.dynamic_index_in_dim(pair, y, 0, keepdims=False)
    other = lax.dynamic_index_in_dim(pair, 1 - y, 0, keepdims=False)
    return [own, ring_shift(other, 1), ring_shift(other, 3), ring_shift(own, 2)]


def body(
    tokens,
    cotangent,
    seq_lengths,
    seq_device,
    in_weight,
    conv_kernel,
    out_weight,
    norm_gain,
    gate_weight,
    up_weight,
    down_weight,
    moment_in,
    moment_conv,
    moment_out,
    moment_gain,
    moment_gate,
    moment_up,
    moment_down,
    square_in,
    square_conv,
    square_out,
    square_gain,
    square_gate,
    square_up,
    square_down,
):
    masters = (in_weight, conv_kernel, out_weight, norm_gain, gate_weight, up_weight, down_weight)
    moments = (moment_in, moment_conv, moment_out, moment_gain, moment_gate, moment_up, moment_down)
    squares = (square_in, square_conv, square_out, square_gain, square_gate, square_up, square_down)
    rep, z, x, y, core = [lax.axis_index(name) for name in AXES]
    device = (((rep * SIDE + z) * SIDE + x) * 2 + y) * 2 + core
    slots, width = tokens.shape
    rows = in_weight.shape[0]
    hidden_units = gate_weight.shape[1]
    half = hidden_units // 2
    down_rows = down_weight.shape[0]
    chips = SIDE * SIDE
    tap_count = conv_kernel.shape[1]
    channels = width // 2
    in_columns = 3 * channels
    lanes = width // 2
    mix_columns = in_columns + AUX + lanes

    segment, live_rows = layout(seq_lengths, seq_device, device, slots)
    core_device = device + 1 - 2 * core
    core_segment, _ = layout(seq_lengths, seq_device, core_device, slots)
    segment = jnp.concatenate([segment, core_segment + seq_lengths.shape[0] + 1])
    live_float = wide(live_rows)[:, None]
    places = plane_places(z, x, core)

    def by_core(weight, groups, run):
        return low(weight).reshape(rows, groups, -1, 2, run)

    in_split = by_core(in_weight, 3, rows)
    gate_split, up_split = by_core(gate_weight, 1, down_rows), by_core(up_weight, 1, down_rows)
    small = jnp.concatenate([conv_kernel, norm_gain[:, None]], axis=1)
    small = jnp.pad(low(small), ((0, 0), (0, AUX - tap_count - 1)))

    def core_rows(parts, common):
        shares = [
            jnp.concatenate([p[..., which, :].reshape(rows, -1) for p in parts] + common, axis=1)
            for which in range(2)
        ]
        mine = jnp.where(core == 0, shares[0], shares[1])
        theirs = jnp.where(core == 0, shares[1], shares[0])
        return in_order(core, mine, core_swap(theirs))

    out_low = low(out_weight)
    out_rows = jnp.concatenate([out_low[:, :lanes], out_low[:, lanes:]], axis=0)
    gather_index = jnp.concatenate([places, jnp.stack([y, 1 - y]).astype(jnp.int32)])

    mix_rows = jnp.concatenate([core_rows([in_split], [small]), out_rows], axis=1)
    mix_first = [mix_rows] + [plane_shift(mix_rows, d, 0) for d in (1, 2, 3)]
    mix_joined = jnp.concatenate(mix_first, axis=0)
    mix_second = [plane_shift(mix_joined, d, 1) for d in (1, 2, 3)]
    mix_own = jnp.concatenate([mix_joined] + mix_second, axis=0)
    mix_w = spread_blocks(
        [part.reshape(chips, 2 * rows, mix_columns) for part in (mix_own, ring_turn(mix_own))],
        gather_index,
        jax.ShapeDtypeStruct((chips, 2, 2 * rows, mix_columns), jnp.bfloat16),
        lambda d, k, index: (index[k], index[chips + d]),
    ).reshape(width, mix_columns)
    in_w = mix_w[:, :in_columns]
    out_w = mix_w[:, mix_columns - lanes :].reshape(chips * 2, 2, rows, lanes)
    out_w = jnp.concatenate([out_w[:, 0], out_w[:, 1]], axis=2).reshape(channels, width)
    small_w = wide(mix_w[:, in_columns : in_columns + tap_count + 1]).T
    core_taps = small_w[:tap_count].reshape(tap_count, -1, 2, rows)
    core_taps = jnp.where(core == 0, core_taps[:, :, 0], core_taps[:, :, 1])
    core_taps = core_taps.reshape(tap_count, channels)
    taps = [core_taps[k] for k in range(tap_count)]
    gain = small_w[tap_count]

    unit_rows = core_rows([gate_split, up_split], [])
    unit_pair = after(in_order(y, unit_rows, pair_swap(unit_rows)), *mix_first)
    unit_first = [unit_pair] + [plane_shift(unit_pair, d, 0) for d in (1, 2, 3)]
    unit_joined = after(jnp.concatenate(unit_first, axis=0), *mix_second)
    unit_own = [unit_joined] + [plane_shift(unit_joined, d, 1) for d in (1, 2, 3)]
    unit_w = spread_blocks(
        [part.reshape(SIDE, SIDE * rows, 2 * half) for part in unit_own],
        places,
        jax.ShapeDtypeStruct((chips, SIDE * rows, 2 * half), jnp.bfloat16),
        lambda d, k, index: index[d * SIDE + k],
    ).reshape(width, 2 * half)
    down_low = low(down_weight)
    down_pair = after(in_order(y, down_low, pair_swap(down_low)), *unit_first)
    down_first = [down_pair] + [plane_shift(down_pair, d, 0) for d in (1, 2, 3)]
    down_joined = after(jnp.concatenate(down_first, axis=0), *unit_own)
    down_own = [down_joined] + [plane_shift(down_joined, d, 1) for d in (1, 2, 3)]
    down_w = spread_blocks(
        [part.reshape(SIDE, 2 * down_rows, width) for part in down_own],
        places,
        jax.ShapeDtypeStruct((chips, 2 * down_rows, width), jnp.bfloat16),
        lambda d, k, index: index[d * SIDE + k],
    ).reshape(half, width)

    def own_rows_sum(part):
        return part[:slots] + wide(core_swap(low(part[slots:])))

    tokens_both = jnp.concatenate([tokens, core_swap(tokens)], axis=0)
    projected = product(tokens_both, in_w)
    b_branch = projected[:, :channels]
    c_branch = projected[:, channels : 2 * channels]
    x_branch = projected[:, 2 * channels :]
    mixed = b_branch * x_branch
    convolved, matches = conv_forward(mixed, taps, segment)
    conv_low = low(c_branch * convolved)
    hidden = wide(tokens) + own_rows_sum(product(conv_low, out_w))
    inv_rms = lax.rsqrt(jnp.mean(hidden * hidden, axis=-1, keepdims=True) + NORM_EPS)
    scaled = hidden * inv_rms
    normed = low(scaled * gain)

    grad_out = wide(cotangent) * live_float
    grad_low = low(grad_out)
    grad_both = jnp.concatenate([grad_low, core_swap(grad_low)], axis=0)
    normed_both = jnp.concatenate([normed, core_swap(normed)], axis=0)
    pre = product(normed_both, unit_w)
    gate_pre, up_pre = pre[:, :half], pre[:, half:]
    sigmoid_gate = jax.nn.sigmoid(gate_pre)
    silu_gate = gate_pre * sigmoid_gate
    act_low = low(silu_gate * up_pre)
    ffn_part = product(act_low, down_w)
    grad_act = product_nt(grad_both, down_w)
    grad_up = low(grad_act * silu_gate)
    grad_gate = low(grad_act * up_pre * sigmoid_gate * (1.0 + gate_pre * (1.0 - sigmoid_gate)))
    sources = plane_sources(z, x, core)

    grad_down = low(product_tn(act_low, grad_both)).reshape(chips, 2 * down_rows, width)
    down_messages = pick_blocks(grad_down, sources)
    down_parts = plane_first(down_messages)

    unit_grads = [
        low(product_tn(after(normed_both, *down_messages), part)).reshape(chips, 2, 2 * rows, half)
        for part in (grad_gate, grad_up)
    ]

    def of_parity(which):
        picked = [lax.dynamic_index_in_dim(g, which, 1, keepdims=False) for g in unit_grads]
        return jnp.concatenate(picked, axis=2)

    unit_sent = of_parity(1 - y)
    unit_other = ring_turn(unit_sent)
    norm_part = product_nt(grad_gate, unit_w[:, :half]) + product_nt(grad_up, unit_w[:, half:])
    grad_norm = own_rows_sum(norm_part)
    unit_blocks = low(wide(of_parity(y)) + wide(unit_other))

    grad_gain = jnp.sum(grad_norm * scaled, axis=0)
    weighted = grad_norm * gain
    grad_hidden = (
        grad_out
        + inv_rms * weighted
        - scaled * inv_rms * inv_rms * jnp.mean(weighted * hidden, axis=-1, keepdims=True)
    )
    grad_mix = low(grad_hidden)
    mix_both = jnp.concatenate([grad_mix, core_swap(grad_mix)], axis=0)
    grad_conv_out = product_nt(mix_both, out_w)
    grad_out_w = low(product_tn(conv_low, mix_both))
    grad_c = grad_conv_out * convolved
    grad_conv = grad_conv_out * c_branch
    grad_mixed, grad_taps = conv_backward(grad_conv, mixed, taps, matches)
    grad_proj = low(jnp.concatenate([grad_mixed * x_branch, grad_c, grad_mixed * b_branch], axis=1))
    grad_in = low(product_tn(tokens_both, grad_proj))

    core_taps = jnp.stack(grad_taps, axis=0).reshape(tap_count, -1, 1, rows)
    is_core = lax.broadcasted_iota(jnp.int32, (1, 1, 2, 1), 2) == core
    grad_small = jnp.where(is_core, core_taps, 0.0).reshape(tap_count, width)
    grad_small = jnp.concatenate([grad_small, grad_gain[None]], axis=0)
    grad_small = jnp.pad(low(grad_small), ((0, AUX - tap_count - 1), (0, 0))).T
    out_blocks = grad_out_w.reshape(chips * 2, rows, width)
    out_blocks = jnp.concatenate([out_blocks[..., :lanes], out_blocks[..., lanes:]], axis=1)
    mix_blocks = jnp.concatenate([grad_in, grad_small, out_blocks.reshape(width, lanes)], axis=1)
    mix_blocks = after(mix_blocks.reshape(chips, SIDE * rows, mix_columns), unit_sent)
    mix_messages = pick_blocks(mix_blocks, sources)
    mix_parts = plane_first(mix_messages)
    input_part = product_nt(after(grad_proj, *mix_messages), in_w)
    input_grad = grad_hidden + own_rows_sum(input_part)

    unit_messages = pick_blocks(after(unit_blocks, *mix_messages), sources)
    ffn_out = own_rows_sum(ffn_part)
    block_out = low((hidden + ffn_out) * live_float)

    mix_parts = [after(part, unit_other) for part in mix_parts]
    down_sum = low(sum_wide(plane_second(down_parts, z, x, core)))
    total_down = sum_wide(ring_parts(down_sum.reshape(2, down_rows, width), y))

    unit_parts = plane_first(unit_messages)
    unit_sum = low(sum_wide(plane_second(unit_parts, z, x, core))).reshape(2, rows, 2 * half)
    own = lax.dynamic_index_in_dim(unit_sum, core, 0, keepdims=False)
    other = lax.dynamic_index_in_dim(unit_sum, 1 - core, 0, keepdims=False)
    own_units = wide(own) + wide(ring_shift(own, 2))
    other_units = wide(ring_shift(other, 0, 1)) + wide(ring_shift(other, 2, 1))
    unit_zero = jnp.where(core == 0, own_units, other_units)
    unit_one = jnp.where(core == 0, other_units, own_units)

    def merge(first, second):
        pair = [part.reshape(rows, -1, down_rows) for part in (first, second)]
        return jnp.stack(pair, axis=2).reshape(rows, hidden_units)

    total_gate = merge(unit_zero[:, :half], unit_one[:, :half])
    total_up = merge(unit_zero[:, half:], unit_one[:, half:])

    mix_sum = low(sum_wide(plane_second(mix_parts, z, x, core)))
    mix_terms = ring_parts(mix_sum.reshape(2, 2 * rows, mix_columns), y)

    def mix_total(start, size):
        return sum_wide([lax.slice_in_dim(term, start, start + size, axis=1) for term in mix_terms])

    in_total = mix_total(0, in_columns + AUX).reshape(2, rows, in_columns + AUX)
    own_in = lax.dynamic_index_in_dim(in_total, core, 0, keepdims=False)
    other_in = core_swap(lax.dynamic_index_in_dim(in_total, 1 - core, 0, keepdims=False))
    halves = [part[:, :in_columns].reshape(rows, 3, -1, rows) for part in (own_in, other_in)]
    in_zero = jnp.where(core == 0, halves[0], halves[1])
    in_one = jnp.where(core == 0, halves[1], halves[0])
    total_in = jnp.stack([in_zero, in_one], axis=3).reshape(rows, 3 * width)
    out_total = mix_total(in_columns + AUX, lanes)
    total_out = jnp.concatenate([out_total[:rows], out_total[rows:]], axis=1)
    total_small = own_in[:, in_columns:] + other_in[:, in_columns:]
    lane = lax.broadcasted_iota(jnp.int32, total_small.shape, 1)
    small_columns = [
        jnp.sum(jnp.where(lane == k, total_small, 0.0), axis=1) for k in range(tap_count + 1)
    ]
    gradients = (
        total_in,
        jnp.stack(small_columns[:tap_count], axis=1),
        total_out,
        small_columns[tap_count],
        total_gate,
        total_up,
        total_down,
    )
    bias_one = 1.0 - BETA_ONE**STEP
    bias_two = 1.0 - BETA_TWO**STEP
    updated = []
    firsts = []
    seconds = []
    for master, moment, variance, gradient, step_rate, decay_rate in zip(
        masters, moments, squares, gradients, STEP_RATES, DECAY_RATES
    ):
        first_new = BETA_ONE * moment + (1.0 - BETA_ONE) * gradient
        second_new = BETA_TWO * variance + (1.0 - BETA_TWO) * gradient * gradient
        normalized = first_new / bias_one / (jnp.sqrt(second_new / bias_two) + ADAM_EPS)
        updated.append(master - step_rate * (normalized + decay_rate * master))
        firsts.append(first_new)
        seconds.append(second_new)
    return (block_out, input_grad, *updated, *firsts, *seconds)


def solution(mesh):
    grid = Mesh(mesh.devices.reshape(2, SIDE, SIDE, 2, 2), AXES)
    by_token = P(AXES, None)
    matrix, vector = P(SHARD, None), P(SHARD)
    group = (matrix, matrix, matrix, vector, matrix, matrix, matrix)
    return jax.shard_map(
        body,
        mesh=grid,
        in_specs=(by_token, by_token, P(), P(), *group, *group, *group),
        out_specs=(by_token, by_token, *group, *group, *group),
        check_vma=False,
    )
```

```python
import jax
import jax.numpy as jnp
from jax import lax
from jax.experimental import pallas as pl
from jax.experimental.pallas import tpu as pltpu
from jax.sharding import Mesh
from jax.sharding import PartitionSpec as P

STEP = 10
NORM_EPS = 1e-05
BETA_ONE = 0.9
BETA_TWO = 0.95
ADAM_EPS = 1e-08
STEP_RATES = (0.02, 0.3, 0.02, 0.3, 0.02, 0.02, 0.02)
DECAY_RATES = (0.1, 0.0, 0.1, 0.0, 0.1, 0.1, 0.1)

AXES = ("rep", "z", "x", "y", "core")
SHARD = ("z", "x", "y", "core")
SIDE = 4
AUX = 128


def layout(seq_lengths, seq_device, device, row_count):
    owned_len = jnp.where(seq_device == device, seq_lengths, 0)
    seq_ends = jnp.cumsum(owned_len, dtype=jnp.int32)
    slot_index = jnp.arange(row_count, dtype=jnp.int32)
    segment = jnp.sum(
        (seq_ends[None, :] <= slot_index[:, None]).astype(jnp.int32), axis=1, dtype=jnp.int32
    )
    live_rows = (slot_index < seq_ends[-1]).astype(jnp.int32)
    return (segment, live_rows)


def product(left, right):
    return jnp.dot(left, right, preferred_element_type=jnp.float32)


def product_nt(left, right):
    return lax.dot_general(
        left, right, (((1,), (1,)), ((), ())), preferred_element_type=jnp.float32
    )


def product_tn(left, right):
    return lax.dot_general(
        left, right, (((0,), (0,)), ((), ())), preferred_element_type=jnp.float32
    )


def conv_forward(mixed, taps, segment):
    summed = mixed * taps[0]
    matches = []
    for offset in range(1, len(taps)):
        earlier = jnp.pad(mixed, ((offset, 0), (0, 0)))[:-offset]
        same_seq = (jnp.pad(segment, (offset, 0), constant_values=-1)[:-offset] == segment)[:, None]
        matches.append(same_seq)
        summed = summed + jnp.where(same_seq, earlier * taps[offset], 0.0)
    return (summed, matches)


def conv_backward(gradient, mixed, taps, matches):
    grad_mixed = gradient * taps[0]
    grad_taps = [jnp.sum(gradient * mixed, axis=0)]
    for offset in range(1, len(taps)):
        masked = jnp.where(matches[offset - 1], gradient, 0.0)
        later = jnp.pad(masked, ((0, offset), (0, 0)))[offset:]
        grad_mixed = grad_mixed + later * taps[offset]
        earlier = jnp.pad(mixed, ((offset, 0), (0, 0)))[:-offset]
        grad_taps.append(jnp.sum(masked * earlier, axis=0))
    return (grad_mixed, grad_taps)


def low(value):
    return value.astype(jnp.bfloat16)


def wide(value):
    return value.astype(jnp.float32)


def after(value, *earlier):
    return lax.optimization_barrier((value,) + earlier)[0]


def plane_shift(value, distance, turn):
    pairs = []
    for z in range(SIDE):
        for x in range(SIDE):
            for core in range(2):
                if (core + turn) % 2 == 0:
                    to_z, to_x = z, (x + distance) % SIDE
                else:
                    to_z, to_x = (z + distance) % SIDE, x
                pairs.append(((z * SIDE + x) * 2 + core, (to_z * SIDE + to_x) * 2 + core))
    return lax.ppermute(value, ("z", "x", "core"), pairs)


def ring_shift(value, distance, swap=0):
    pairs = []
    for y in range(SIDE):
        for core in range(2):
            pairs.append((y * 2 + core, (y + distance) % SIDE * 2 + (core + swap) % 2))
    return lax.ppermute(value, ("rep", "y", "core"), pairs)


def ring_turn(value):
    pairs = []
    for y in range(SIDE):
        for core in range(2):
            pairs.append((y * 2 + core, (y + 1 - 2 * core) % SIDE * 2 + core))
    return lax.ppermute(value, ("rep", "y", "core"), pairs)


def core_swap(value):
    return lax.ppermute(value, "core", [(0, 1), (1, 0)])


def pair_swap(value):
    return lax.ppermute(value, "y", [(0, 1), (1, 0)])


def in_order(index, mine, other):
    first = jnp.where(index == 0, mine, other)
    second = jnp.where(index == 0, other, mine)
    return jnp.concatenate([first, second], axis=0)


def copy_kernel(loads, stores):
    def kernel(index_ref, *refs):
        load_sems, store_sems = refs[-2:]
        fills = [
            pltpu.make_async_copy(source, target, load_sems.at[i])
            for i, (source, target) in enumerate(loads(index_ref, refs))
        ]
        for fill in fills:
            fill.start()
        empties = []
        for i, (needs, source, target) in enumerate(stores(index_ref, refs)):
            for need in needs:
                fills[need].wait()
            empties.append(pltpu.make_async_copy(source, target, store_sems.at[i]))
            empties[-1].start()
        for empty in empties:
            empty.wait()

    return kernel


def copy_call(kernel, index, sources, out_shapes, scratch, load_count, store_count):
    moved = 2 * sum(source.size * source.dtype.itemsize for source in sources)
    return pl.pallas_call(
        kernel,
        out_shape=out_shapes,
        in_specs=[pl.BlockSpec(memory_space=pltpu.SMEM)]
        + [pl.BlockSpec(memory_space=pl.ANY)] * len(sources),
        out_specs=[pl.BlockSpec(memory_space=pl.ANY)] * len(out_shapes),
        scratch_shapes=scratch
        + [pltpu.SemaphoreType.DMA((load_count,)), pltpu.SemaphoreType.DMA((store_count,))],
        compiler_params=pltpu.CompilerParams(vmem_limit_bytes=40 * 1024 * 1024),
        cost_estimate=pl.CostEstimate(flops=0, bytes_accessed=moved, transcendentals=0),
    )(index, *sources)


def spread_blocks(sources, index, out_shape, place):
    count, blocks = len(sources), sources[0].shape[0]

    def loads(index_ref, refs):
        return [(refs[d], refs[count + 1].at[d]) for d in range(count)]

    def stores(index_ref, refs):
        moves = []
        for d in range(count):
            for k in range(blocks):
                needs = [d] if k == 0 else []
                target = refs[count].at[place(d, k, index_ref)]
                moves.append((needs, refs[count + 1].at[d, k], target))
        return moves

    scratch = [pltpu.VMEM((count,) + sources[0].shape, sources[0].dtype)]
    (out,) = copy_call(
        copy_kernel(loads, stores), index, sources, [out_shape], scratch, count, count * blocks
    )
    return out


def pick_blocks(source, index):
    shape = (SIDE,) + source.shape[1:]

    def loads(index_ref, refs):
        return [
            (refs[0].at[index_ref[d * SIDE + k]], refs[1 + SIDE].at[d, k])
            for d in range(SIDE)
            for k in range(SIDE)
        ]

    def stores(index_ref, refs):
        return [
            (range(d * SIDE, (d + 1) * SIDE), refs[1 + SIDE].at[d], refs[1 + d])
            for d in range(SIDE)
        ]

    return copy_call(
        copy_kernel(loads, stores),
        index,
        [source],
        [jax.ShapeDtypeStruct(shape, source.dtype)] * SIDE,
        [pltpu.VMEM((SIDE,) + shape, source.dtype)],
        SIDE * SIDE,
        SIDE,
    )


def plane_places(z, x, core):
    places = []
    for d2 in range(SIDE):
        for d1 in range(SIDE):
            at_z = jnp.where(core == 0, (z - d2) % SIDE, (z - d1) % SIDE)
            at_x = jnp.where(core == 0, (x - d1) % SIDE, (x - d2) % SIDE)
            places.append(at_z * SIDE + at_x)
    return jnp.stack(places).astype(jnp.int32)


def plane_sources(z, x, core):
    picks = []
    for d in range(SIDE):
        for k in range(SIDE):
            at_z = jnp.where(core == 0, (z + d) % SIDE, k)
            at_x = jnp.where(core == 0, k, (x + d) % SIDE)
            picks.append(at_z * SIDE + at_x)
    return jnp.stack(picks).astype(jnp.int32)


def sum_wide(parts):
    total = wide(parts[0])
    for part in parts[1:]:
        total = total + wide(part)
    return total


def plane_first(messages):
    return [messages[0]] + [plane_shift(messages[d], d, 1) for d in (1, 2, 3)]


def plane_second(parts, z, x, core):
    summed = low(sum_wide(parts))
    me = jnp.where(core == 0, x, z)
    pick = lambda d: lax.dynamic_index_in_dim(summed, (me + d) % SIDE, 0, keepdims=False)
    return [pick(0)] + [plane_shift(pick(d), d, 0) for d in (1, 2, 3)]


def ring_parts(pair, y):
    own = lax.dynamic_index_in_dim(pair, y, 0, keepdims=False)
    other = lax.dynamic_index_in_dim(pair, 1 - y, 0, keepdims=False)
    return [own, ring_shift(other, 1), ring_shift(other, 3), ring_shift(own, 2)]


def body(
    tokens,
    cotangent,
    seq_lengths,
    seq_device,
    in_weight,
    conv_kernel,
    out_weight,
    norm_gain,
    gate_weight,
    up_weight,
    down_weight,
    moment_in,
    moment_conv,
    moment_out,
    moment_gain,
    moment_gate,
    moment_up,
    moment_down,
    square_in,
    square_conv,
    square_out,
    square_gain,
    square_gate,
    square_up,
    square_down,
):
    masters = (in_weight, conv_kernel, out_weight, norm_gain, gate_weight, up_weight, down_weight)
    moments = (moment_in, moment_conv, moment_out, moment_gain, moment_gate, moment_up, moment_down)
    squares = (square_in, square_conv, square_out, square_gain, square_gate, square_up, square_down)
    rep, z, x, y, core = [lax.axis_index(name) for name in AXES]
    device = (((rep * SIDE + z) * SIDE + x) * 2 + y) * 2 + core
    slots, width = tokens.shape
    rows = in_weight.shape[0]
    hidden_units = gate_weight.shape[1]
    half = hidden_units // 2
    down_rows = down_weight.shape[0]
    chips = SIDE * SIDE
    tap_count = conv_kernel.shape[1]
    channels = width // 2
    in_columns = 3 * channels
    lanes = width // 2
    mix_columns = in_columns + AUX + lanes

    segment, live_rows = layout(seq_lengths, seq_device, device, slots)
    core_device = device + 1 - 2 * core
    core_segment, _ = layout(seq_lengths, seq_device, core_device, slots)
    segment = jnp.concatenate([segment, core_segment + seq_lengths.shape[0] + 1])
    live_float = wide(live_rows)[:, None]
    places = plane_places(z, x, core)

    def by_core(weight, groups, run):
        return low(weight).reshape(rows, groups, -1, 2, run)

    in_split = by_core(in_weight, 3, rows)
    gate_split, up_split = by_core(gate_weight, 1, down_rows), by_core(up_weight, 1, down_rows)
    small = jnp.concatenate([conv_kernel, norm_gain[:, None]], axis=1)
    small = jnp.pad(low(small), ((0, 0), (0, AUX - tap_count - 1)))

    def core_rows(parts, common):
        shares = [
            jnp.concatenate([p[..., which, :].reshape(rows, -1) for p in parts] + common, axis=1)
            for which in range(2)
        ]
        mine = jnp.where(core == 0, shares[0], shares[1])
        theirs = jnp.where(core == 0, shares[1], shares[0])
        return in_order(core, mine, core_swap(theirs))

    out_low = low(out_weight)
    out_rows = jnp.concatenate([out_low[:, :lanes], out_low[:, lanes:]], axis=0)
    gather_index = jnp.concatenate([places, jnp.stack([y, 1 - y]).astype(jnp.int32)])

    mix_rows = jnp.concatenate([core_rows([in_split], [small]), out_rows], axis=1)
    mix_first = [mix_rows] + [plane_shift(mix_rows, d, 0) for d in (1, 2, 3)]
    mix_joined = jnp.concatenate(mix_first, axis=0)
    mix_second = [plane_shift(mix_joined, d, 1) for d in (1, 2, 3)]
    mix_own = jnp.concatenate([mix_joined] + mix_second, axis=0)
    mix_w = spread_blocks(
        [part.reshape(chips, 2 * rows, mix_columns) for part in (mix_own, ring_turn(mix_own))],
        gather_index,
        jax.ShapeDtypeStruct((chips, 2, 2 * rows, mix_columns), jnp.bfloat16),
        lambda d, k, index: (index[k], index[chips + d]),
    ).reshape(width, mix_columns)
    in_w = mix_w[:, :in_columns]
    out_w = mix_w[:, mix_columns - lanes :].reshape(chips * 2, 2, rows, lanes)
    out_w = jnp.concatenate([out_w[:, 0], out_w[:, 1]], axis=2).reshape(channels, width)
    small_w = wide(mix_w[:, in_columns : in_columns + tap_count + 1]).T
    core_taps = small_w[:tap_count].reshape(tap_count, -1, 2, rows)
    core_taps = jnp.where(core == 0, core_taps[:, :, 0], core_taps[:, :, 1])
    core_taps = core_taps.reshape(tap_count, channels)
    taps = [core_taps[k] for k in range(tap_count)]
    gain = small_w[tap_count]

    unit_rows = core_rows([gate_split, up_split], [])
    unit_pair = after(in_order(y, unit_rows, pair_swap(unit_rows)), *mix_first)
    unit_first = [unit_pair] + [plane_shift(unit_pair, d, 0) for d in (1, 2, 3)]
    unit_joined = after(jnp.concatenate(unit_first, axis=0), *mix_second)
    unit_own = [unit_joined] + [plane_shift(unit_joined, d, 1) for d in (1, 2, 3)]
    unit_w = spread_blocks(
        [part.reshape(SIDE, SIDE * rows, 2 * half) for part in unit_own],
        places,
        jax.ShapeDtypeStruct((chips, SIDE * rows, 2 * half), jnp.bfloat16),
        lambda d, k, index: index[d * SIDE + k],
    ).reshape(width, 2 * half)
    down_low = low(down_weight)
    down_pair = after(in_order(y, down_low, pair_swap(down_low)), *unit_first)
    down_first = [down_pair] + [plane_shift(down_pair, d, 0) for d in (1, 2, 3)]
    down_joined = after(jnp.concatenate(down_first, axis=0), *unit_own)
    down_own = [down_joined] + [plane_shift(down_joined, d, 1) for d in (1, 2, 3)]
    down_w = spread_blocks(
        [part.reshape(SIDE, 2 * down_rows, width) for part in down_own],
        places,
        jax.ShapeDtypeStruct((chips, 2 * down_rows, width), jnp.bfloat16),
        lambda d, k, index: index[d * SIDE + k],
    ).reshape(half, width)

    def own_rows_sum(part):
        return part[:slots] + wide(core_swap(low(part[slots:])))

    tokens_both = jnp.concatenate([tokens, core_swap(tokens)], axis=0)
    projected = product(tokens_both, in_w)
    b_branch = projected[:, :channels]
    c_branch = projected[:, channels : 2 * channels]
    x_branch = projected[:, 2 * channels :]
    mixed = b_branch * x_branch
    convolved, matches = conv_forward(mixed, taps, segment)
    conv_low = low(c_branch * convolved)
    hidden = wide(tokens) + own_rows_sum(product(conv_low, out_w))
    inv_rms = lax.rsqrt(jnp.mean(hidden * hidden, axis=-1, keepdims=True) + NORM_EPS)
    scaled = hidden * inv_rms
    normed = low(scaled * gain)

    grad_out = wide(cotangent) * live_float
    grad_low = low(grad_out)
    grad_both = jnp.concatenate([grad_low, core_swap(grad_low)], axis=0)
    normed_both = jnp.concatenate([normed, core_swap(normed)], axis=0)
    pre = product(normed_both, unit_w)
    gate_pre, up_pre = pre[:, :half], pre[:, half:]
    sigmoid_gate = jax.nn.sigmoid(gate_pre)
    silu_gate = gate_pre * sigmoid_gate
    act_low = low(silu_gate * up_pre)
    ffn_part = product(act_low, down_w)
    grad_act = product_nt(grad_both, down_w)
    grad_up = low(grad_act * silu_gate)
    grad_gate = low(grad_act * up_pre * sigmoid_gate * (1.0 + gate_pre * (1.0 - sigmoid_gate)))
    sources = plane_sources(z, x, core)

    grad_down = low(product_tn(act_low, grad_both)).reshape(chips, 2 * down_rows, width)
    down_messages = pick_blocks(grad_down, sources)
    down_parts = plane_first(down_messages)

    unit_grads = [
        low(product_tn(after(normed_both, *down_messages), part)).reshape(chips, 2, 2 * rows, half)
        for part in (grad_gate, grad_up)
    ]

    def of_parity(which):
        picked = [lax.dynamic_index_in_dim(g, which, 1, keepdims=False) for g in unit_grads]
        return jnp.concatenate(picked, axis=2)

    unit_sent = of_parity(1 - y)
    unit_other = ring_turn(unit_sent)
    norm_part = product_nt(grad_gate, unit_w[:, :half]) + product_nt(grad_up, unit_w[:, half:])
    grad_norm = own_rows_sum(norm_part)
    unit_blocks = low(wide(of_parity(y)) + wide(unit_other))

    grad_gain = jnp.sum(grad_norm * scaled, axis=0)
    weighted = grad_norm * gain
    grad_hidden = (
        grad_out
        + inv_rms * weighted
        - scaled * inv_rms * inv_rms * jnp.mean(weighted * hidden, axis=-1, keepdims=True)
    )
    grad_mix = low(grad_hidden)
    mix_both = jnp.concatenate([grad_mix, core_swap(grad_mix)], axis=0)
    grad_conv_out = product_nt(mix_both, out_w)
    grad_out_w = low(product_tn(conv_low, mix_both))
    grad_c = grad_conv_out * convolved
    grad_conv = grad_conv_out * c_branch
    grad_mixed, grad_taps = conv_backward(grad_conv, mixed, taps, matches)
    grad_proj = low(jnp.concatenate([grad_mixed * x_branch, grad_c, grad_mixed * b_branch], axis=1))
    grad_in = low(product_tn(tokens_both, grad_proj))

    core_taps = jnp.stack(grad_taps, axis=0).reshape(tap_count, -1, 1, rows)
    is_core = lax.broadcasted_iota(jnp.int32, (1, 1, 2, 1), 2) == core
    grad_small = jnp.where(is_core, core_taps, 0.0).reshape(tap_count, width)
    grad_small = jnp.concatenate([grad_small, grad_gain[None]], axis=0)
    grad_small = jnp.pad(low(grad_small), ((0, AUX - tap_count - 1), (0, 0))).T
    out_blocks = grad_out_w.reshape(chips * 2, rows, width)
    out_blocks = jnp.concatenate([out_blocks[..., :lanes], out_blocks[..., lanes:]], axis=1)
    mix_blocks = jnp.concatenate([grad_in, grad_small, out_blocks.reshape(width, lanes)], axis=1)
    mix_blocks = after(mix_blocks.reshape(chips, SIDE * rows, mix_columns), unit_sent)
    mix_messages = pick_blocks(mix_blocks, sources)
    mix_parts = plane_first(mix_messages)

    unit_messages = pick_blocks(after(unit_blocks, *mix_messages), sources)
    ffn_out = own_rows_sum(ffn_part)
    block_out = low((hidden + ffn_out) * live_float)

    down_sum = low(sum_wide(plane_second(down_parts, z, x, core)))

    unit_parts = plane_first(unit_messages)
    mix_parts = [after(part, *unit_parts) for part in mix_parts]
    input_part = product_nt(after(grad_proj, *unit_parts), in_w)
    input_grad = grad_hidden + own_rows_sum(input_part)
    down_sum = after(down_sum, *unit_parts)
    total_down = sum_wide(ring_parts(down_sum.reshape(2, down_rows, width), y))
    unit_sum = low(sum_wide(plane_second(unit_parts, z, x, core))).reshape(2, rows, 2 * half)
    own = lax.dynamic_index_in_dim(unit_sum, core, 0, keepdims=False)
    other = lax.dynamic_index_in_dim(unit_sum, 1 - core, 0, keepdims=False)
    own_units = wide(own) + wide(ring_shift(own, 2))
    other_units = wide(ring_shift(other, 0, 1)) + wide(ring_shift(other, 2, 1))
    unit_zero = jnp.where(core == 0, own_units, other_units)
    unit_one = jnp.where(core == 0, other_units, own_units)

    def merge(first, second):
        pair = [part.reshape(rows, -1, down_rows) for part in (first, second)]
        return jnp.stack(pair, axis=2).reshape(rows, hidden_units)

    total_gate = merge(unit_zero[:, :half], unit_one[:, :half])
    total_up = merge(unit_zero[:, half:], unit_one[:, half:])

    mix_sum = low(sum_wide(plane_second(mix_parts, z, x, core)))
    mix_terms = ring_parts(mix_sum.reshape(2, 2 * rows, mix_columns), y)

    def mix_total(start, size):
        return sum_wide([lax.slice_in_dim(term, start, start + size, axis=1) for term in mix_terms])

    in_total = mix_total(0, in_columns + AUX).reshape(2, rows, in_columns + AUX)
    own_in = lax.dynamic_index_in_dim(in_total, core, 0, keepdims=False)
    other_in = core_swap(lax.dynamic_index_in_dim(in_total, 1 - core, 0, keepdims=False))
    halves = [part[:, :in_columns].reshape(rows, 3, -1, rows) for part in (own_in, other_in)]
    in_zero = jnp.where(core == 0, halves[0], halves[1])
    in_one = jnp.where(core == 0, halves[1], halves[0])
    total_in = jnp.stack([in_zero, in_one], axis=3).reshape(rows, 3 * width)
    out_total = mix_total(in_columns + AUX, lanes)
    total_out = jnp.concatenate([out_total[:rows], out_total[rows:]], axis=1)
    total_small = own_in[:, in_columns:] + other_in[:, in_columns:]
    lane = lax.broadcasted_iota(jnp.int32, total_small.shape, 1)
    small_columns = [
        jnp.sum(jnp.where(lane == k, total_small, 0.0), axis=1) for k in range(tap_count + 1)
    ]
    gradients = (
        total_in,
        jnp.stack(small_columns[:tap_count], axis=1),
        total_out,
        small_columns[tap_count],
        total_gate,
        total_up,
        total_down,
    )
    bias_one = 1.0 - BETA_ONE**STEP
    bias_two = 1.0 - BETA_TWO**STEP
    updated = []
    firsts = []
    seconds = []
    for master, moment, variance, gradient, step_rate, decay_rate in zip(
        masters, moments, squares, gradients, STEP_RATES, DECAY_RATES
    ):
        first_new = BETA_ONE * moment + (1.0 - BETA_ONE) * gradient
        second_new = BETA_TWO * variance + (1.0 - BETA_TWO) * gradient * gradient
        normalized = first_new / bias_one / (jnp.sqrt(second_new / bias_two) + ADAM_EPS)
        updated.append(master - step_rate * (normalized + decay_rate * master))
        firsts.append(first_new)
        seconds.append(second_new)
    return (block_out, input_grad, *updated, *firsts, *seconds)


def solution(mesh):
    grid = Mesh(mesh.devices.reshape(2, SIDE, SIDE, 2, 2), AXES)
    by_token = P(AXES, None)
    matrix, vector = P(SHARD, None), P(SHARD)
    group = (matrix, matrix, matrix, vector, matrix, matrix, matrix)
    return jax.shard_map(
        body,
        mesh=grid,
        in_specs=(by_token, by_token, P(), P(), *group, *group, *group),
        out_specs=(by_token, by_token, *group, *group, *group),
        check_vma=False,
    )
```

```python
import jax
import jax.numpy as jnp
from jax import lax
from jax.experimental import pallas as pl
from jax.experimental.pallas import tpu as pltpu
from jax.sharding import Mesh
from jax.sharding import PartitionSpec as P

STEP = 10
NORM_EPS = 1e-05
BETA_ONE = 0.9
BETA_TWO = 0.95
ADAM_EPS = 1e-08
STEP_RATES = (0.02, 0.3, 0.02, 0.3, 0.02, 0.02, 0.02)
DECAY_RATES = (0.1, 0.0, 0.1, 0.0, 0.1, 0.1, 0.1)

AXES = ("rep", "z", "x", "y", "core")
SHARD = ("z", "x", "y", "core")
SIDE = 4
AUX = 128


def layout(seq_lengths, seq_device, device, row_count):
    owned_len = jnp.where(seq_device == device, seq_lengths, 0)
    seq_ends = jnp.cumsum(owned_len, dtype=jnp.int32)
    slot_index = jnp.arange(row_count, dtype=jnp.int32)
    segment = jnp.sum(
        (seq_ends[None, :] <= slot_index[:, None]).astype(jnp.int32), axis=1, dtype=jnp.int32
    )
    live_rows = (slot_index < seq_ends[-1]).astype(jnp.int32)
    return (segment, live_rows)


def product(left, right):
    return jnp.dot(left, right, preferred_element_type=jnp.float32)


def product_nt(left, right):
    return lax.dot_general(
        left, right, (((1,), (1,)), ((), ())), preferred_element_type=jnp.float32
    )


def product_tn(left, right):
    return lax.dot_general(
        left, right, (((0,), (0,)), ((), ())), preferred_element_type=jnp.float32
    )


def conv_forward(mixed, taps, segment):
    summed = mixed * taps[0]
    matches = []
    for offset in range(1, len(taps)):
        earlier = jnp.pad(mixed, ((offset, 0), (0, 0)))[:-offset]
        same_seq = (jnp.pad(segment, (offset, 0), constant_values=-1)[:-offset] == segment)[:, None]
        matches.append(same_seq)
        summed = summed + jnp.where(same_seq, earlier * taps[offset], 0.0)
    return (summed, matches)


def conv_backward(gradient, mixed, taps, matches):
    grad_mixed = gradient * taps[0]
    grad_taps = [jnp.sum(gradient * mixed, axis=0)]
    for offset in range(1, len(taps)):
        masked = jnp.where(matches[offset - 1], gradient, 0.0)
        later = jnp.pad(masked, ((0, offset), (0, 0)))[offset:]
        grad_mixed = grad_mixed + later * taps[offset]
        earlier = jnp.pad(mixed, ((offset, 0), (0, 0)))[:-offset]
        grad_taps.append(jnp.sum(masked * earlier, axis=0))
    return (grad_mixed, grad_taps)


def low(value):
    return value.astype(jnp.bfloat16)


def wide(value):
    return value.astype(jnp.float32)


def after(value, *earlier):
    return lax.optimization_barrier((value,) + earlier)[0]


def plane_shift(value, distance, turn):
    pairs = []
    for z in range(SIDE):
        for x in range(SIDE):
            for core in range(2):
                if (core + turn) % 2 == 0:
                    to_z, to_x = z, (x + distance) % SIDE
                else:
                    to_z, to_x = (z + distance) % SIDE, x
                pairs.append(((z * SIDE + x) * 2 + core, (to_z * SIDE + to_x) * 2 + core))
    return lax.ppermute(value, ("z", "x", "core"), pairs)


def ring_shift(value, distance, swap=0):
    pairs = []
    for y in range(SIDE):
        for core in range(2):
            pairs.append((y * 2 + core, (y + distance) % SIDE * 2 + (core + swap) % 2))
    return lax.ppermute(value, ("rep", "y", "core"), pairs)


def ring_turn(value):
    pairs = []
    for y in range(SIDE):
        for core in range(2):
            pairs.append((y * 2 + core, (y + 1 - 2 * core) % SIDE * 2 + core))
    return lax.ppermute(value, ("rep", "y", "core"), pairs)


def core_swap(value):
    return lax.ppermute(value, "core", [(0, 1), (1, 0)])


def pair_swap(value):
    return lax.ppermute(value, "y", [(0, 1), (1, 0)])


def in_order(index, mine, other):
    first = jnp.where(index == 0, mine, other)
    second = jnp.where(index == 0, other, mine)
    return jnp.concatenate([first, second], axis=0)


def copy_kernel(loads, stores):
    def kernel(index_ref, *refs):
        load_sems, store_sems = refs[-2:]
        fills = [
            pltpu.make_async_copy(source, target, load_sems.at[i])
            for i, (source, target) in enumerate(loads(index_ref, refs))
        ]
        for fill in fills:
            fill.start()
        empties = []
        for i, (needs, source, target) in enumerate(stores(index_ref, refs)):
            for need in needs:
                fills[need].wait()
            empties.append(pltpu.make_async_copy(source, target, store_sems.at[i]))
            empties[-1].start()
        for empty in empties:
            empty.wait()

    return kernel


def copy_call(kernel, index, sources, out_shapes, scratch, load_count, store_count):
    moved = 2 * sum(source.size * source.dtype.itemsize for source in sources)
    return pl.pallas_call(
        kernel,
        out_shape=out_shapes,
        in_specs=[pl.BlockSpec(memory_space=pltpu.SMEM)]
        + [pl.BlockSpec(memory_space=pl.ANY)] * len(sources),
        out_specs=[pl.BlockSpec(memory_space=pl.ANY)] * len(out_shapes),
        scratch_shapes=scratch
        + [pltpu.SemaphoreType.DMA((load_count,)), pltpu.SemaphoreType.DMA((store_count,))],
        compiler_params=pltpu.CompilerParams(vmem_limit_bytes=40 * 1024 * 1024),
        cost_estimate=pl.CostEstimate(flops=0, bytes_accessed=moved, transcendentals=0),
    )(index, *sources)


def spread_blocks(sources, index, out_shape, place):
    count, blocks = len(sources), sources[0].shape[0]

    def loads(index_ref, refs):
        return [(refs[d], refs[count + 1].at[d]) for d in range(count)]

    def stores(index_ref, refs):
        moves = []
        for d in range(count):
            for k in range(blocks):
                needs = [d] if k == 0 else []
                target = refs[count].at[place(d, k, index_ref)]
                moves.append((needs, refs[count + 1].at[d, k], target))
        return moves

    scratch = [pltpu.VMEM((count,) + sources[0].shape, sources[0].dtype)]
    (out,) = copy_call(
        copy_kernel(loads, stores), index, sources, [out_shape], scratch, count, count * blocks
    )
    return out


def pick_blocks(source, index):
    shape = (SIDE,) + source.shape[1:]

    def loads(index_ref, refs):
        return [
            (refs[0].at[index_ref[d * SIDE + k]], refs[1 + SIDE].at[d, k])
            for d in range(SIDE)
            for k in range(SIDE)
        ]

    def stores(index_ref, refs):
        return [
            (range(d * SIDE, (d + 1) * SIDE), refs[1 + SIDE].at[d], refs[1 + d])
            for d in range(SIDE)
        ]

    return copy_call(
        copy_kernel(loads, stores),
        index,
        [source],
        [jax.ShapeDtypeStruct(shape, source.dtype)] * SIDE,
        [pltpu.VMEM((SIDE,) + shape, source.dtype)],
        SIDE * SIDE,
        SIDE,
    )


def plane_places(z, x, core):
    places = []
    for d2 in range(SIDE):
        for d1 in range(SIDE):
            at_z = jnp.where(core == 0, (z - d2) % SIDE, (z - d1) % SIDE)
            at_x = jnp.where(core == 0, (x - d1) % SIDE, (x - d2) % SIDE)
            places.append(at_z * SIDE + at_x)
    return jnp.stack(places).astype(jnp.int32)


def plane_sources(z, x, core):
    picks = []
    for d in range(SIDE):
        for k in range(SIDE):
            at_z = jnp.where(core == 0, (z + d) % SIDE, k)
            at_x = jnp.where(core == 0, k, (x + d) % SIDE)
            picks.append(at_z * SIDE + at_x)
    return jnp.stack(picks).astype(jnp.int32)


def sum_wide(parts):
    total = wide(parts[0])
    for part in parts[1:]:
        total = total + wide(part)
    return total


def plane_first(messages):
    return [messages[0]] + [plane_shift(messages[d], d, 1) for d in (1, 2, 3)]


def plane_second(parts, z, x, core):
    summed = low(sum_wide(parts))
    me = jnp.where(core == 0, x, z)
    pick = lambda d: lax.dynamic_index_in_dim(summed, (me + d) % SIDE, 0, keepdims=False)
    return [pick(0)] + [plane_shift(pick(d), d, 0) for d in (1, 2, 3)]


def ring_parts(pair, y):
    own = lax.dynamic_index_in_dim(pair, y, 0, keepdims=False)
    other = lax.dynamic_index_in_dim(pair, 1 - y, 0, keepdims=False)
    return [own, ring_shift(other, 1), ring_shift(other, 3), ring_shift(own, 2)]


def body(
    tokens,
    cotangent,
    seq_lengths,
    seq_device,
    in_weight,
    conv_kernel,
    out_weight,
    norm_gain,
    gate_weight,
    up_weight,
    down_weight,
    moment_in,
    moment_conv,
    moment_out,
    moment_gain,
    moment_gate,
    moment_up,
    moment_down,
    square_in,
    square_conv,
    square_out,
    square_gain,
    square_gate,
    square_up,
    square_down,
):
    masters = (in_weight, conv_kernel, out_weight, norm_gain, gate_weight, up_weight, down_weight)
    moments = (moment_in, moment_conv, moment_out, moment_gain, moment_gate, moment_up, moment_down)
    squares = (square_in, square_conv, square_out, square_gain, square_gate, square_up, square_down)
    rep, z, x, y, core = [lax.axis_index(name) for name in AXES]
    device = (((rep * SIDE + z) * SIDE + x) * 2 + y) * 2 + core
    slots, width = tokens.shape
    rows = in_weight.shape[0]
    hidden_units = gate_weight.shape[1]
    half = hidden_units // 2
    down_rows = down_weight.shape[0]
    chips = SIDE * SIDE
    tap_count = conv_kernel.shape[1]
    channels = width // 2
    in_columns = 3 * channels
    lanes = width // 2
    mix_columns = in_columns + AUX + lanes

    segment, live_rows = layout(seq_lengths, seq_device, device, slots)
    core_device = device + 1 - 2 * core
    core_segment, _ = layout(seq_lengths, seq_device, core_device, slots)
    segment = jnp.concatenate([segment, core_segment + seq_lengths.shape[0] + 1])
    live_float = wide(live_rows)[:, None]
    places = plane_places(z, x, core)

    def by_core(weight, groups, run):
        return low(weight).reshape(rows, groups, -1, 2, run)

    in_split = by_core(in_weight, 3, rows)
    gate_split, up_split = by_core(gate_weight, 1, down_rows), by_core(up_weight, 1, down_rows)
    small = jnp.concatenate([conv_kernel, norm_gain[:, None]], axis=1)
    small = jnp.pad(low(small), ((0, 0), (0, AUX - tap_count - 1)))

    def core_rows(parts, common):
        shares = [
            jnp.concatenate([p[..., which, :].reshape(rows, -1) for p in parts] + common, axis=1)
            for which in range(2)
        ]
        mine = jnp.where(core == 0, shares[0], shares[1])
        theirs = jnp.where(core == 0, shares[1], shares[0])
        return in_order(core, mine, core_swap(theirs))

    out_low = low(out_weight)
    out_rows = jnp.concatenate([out_low[:, :lanes], out_low[:, lanes:]], axis=0)
    gather_index = jnp.concatenate([places, jnp.stack([y, 1 - y]).astype(jnp.int32)])

    mix_rows = jnp.concatenate([core_rows([in_split], [small]), out_rows], axis=1)
    mix_first = [mix_rows] + [plane_shift(mix_rows, d, 0) for d in (1, 2, 3)]
    mix_joined = jnp.concatenate(mix_first, axis=0)
    mix_second = [plane_shift(mix_joined, d, 1) for d in (1, 2, 3)]
    mix_own = jnp.concatenate([mix_joined] + mix_second, axis=0)
    mix_w = spread_blocks(
        [part.reshape(chips, 2 * rows, mix_columns) for part in (mix_own, ring_turn(mix_own))],
        gather_index,
        jax.ShapeDtypeStruct((chips, 2, 2 * rows, mix_columns), jnp.bfloat16),
        lambda d, k, index: (index[k], index[chips + d]),
    ).reshape(width, mix_columns)
    in_w = mix_w[:, :in_columns]
    out_w = mix_w[:, mix_columns - lanes :].reshape(chips * 2, 2, rows, lanes)
    out_w = jnp.concatenate([out_w[:, 0], out_w[:, 1]], axis=2).reshape(channels, width)
    small_w = wide(mix_w[:, in_columns : in_columns + tap_count + 1]).T
    core_taps = small_w[:tap_count].reshape(tap_count, -1, 2, rows)
    core_taps = jnp.where(core == 0, core_taps[:, :, 0], core_taps[:, :, 1])
    core_taps = core_taps.reshape(tap_count, channels)
    taps = [core_taps[k] for k in range(tap_count)]
    gain = small_w[tap_count]

    unit_rows = core_rows([gate_split, up_split], [])
    unit_pair = after(in_order(y, unit_rows, pair_swap(unit_rows)), *mix_first)
    unit_first = [unit_pair] + [plane_shift(unit_pair, d, 0) for d in (1, 2, 3)]
    unit_joined = after(jnp.concatenate(unit_first, axis=0), *mix_second)
    unit_own = [unit_joined] + [plane_shift(unit_joined, d, 1) for d in (1, 2, 3)]
    unit_w = spread_blocks(
        [part.reshape(SIDE, SIDE * rows, 2 * half) for part in unit_own],
        places,
        jax.ShapeDtypeStruct((chips, SIDE * rows, 2 * half), jnp.bfloat16),
        lambda d, k, index: index[d * SIDE + k],
    ).reshape(width, 2 * half)
    down_low = low(down_weight)
    down_pair = after(in_order(y, down_low, pair_swap(down_low)), *unit_first)
    down_first = [down_pair] + [plane_shift(down_pair, d, 0) for d in (1, 2, 3)]
    down_joined = after(jnp.concatenate(down_first, axis=0), *unit_own)
    down_own = [down_joined] + [plane_shift(down_joined, d, 1) for d in (1, 2, 3)]
    down_w = spread_blocks(
        [part.reshape(SIDE, 2 * down_rows, width) for part in down_own],
        places,
        jax.ShapeDtypeStruct((chips, 2 * down_rows, width), jnp.bfloat16),
        lambda d, k, index: index[d * SIDE + k],
    ).reshape(half, width)

    def own_rows_sum(part):
        return part[:slots] + wide(core_swap(low(part[slots:])))

    tokens_both = jnp.concatenate([tokens, core_swap(tokens)], axis=0)
    projected = product(tokens_both, in_w)
    b_branch = projected[:, :channels]
    c_branch = projected[:, channels : 2 * channels]
    x_branch = projected[:, 2 * channels :]
    mixed = b_branch * x_branch
    convolved, matches = conv_forward(mixed, taps, segment)
    conv_low = low(c_branch * convolved)
    hidden = wide(tokens) + own_rows_sum(product(conv_low, out_w))
    inv_rms = lax.rsqrt(jnp.mean(hidden * hidden, axis=-1, keepdims=True) + NORM_EPS)
    scaled = hidden * inv_rms
    normed = low(scaled * gain)

    grad_out = wide(cotangent) * live_float
    grad_low = low(grad_out)
    grad_both = jnp.concatenate([grad_low, core_swap(grad_low)], axis=0)
    normed_both = jnp.concatenate([normed, core_swap(normed)], axis=0)
    pre = product(normed_both, unit_w)
    gate_pre, up_pre = pre[:, :half], pre[:, half:]
    sigmoid_gate = jax.nn.sigmoid(gate_pre)
    silu_gate = gate_pre * sigmoid_gate
    act_low = low(silu_gate * up_pre)
    ffn_part = product(act_low, down_w)
    grad_act = product_nt(grad_both, down_w)
    grad_up = low(grad_act * silu_gate)
    grad_gate = low(grad_act * up_pre * sigmoid_gate * (1.0 + gate_pre * (1.0 - sigmoid_gate)))
    sources = plane_sources(z, x, core)

    grad_down = low(product_tn(act_low, grad_both)).reshape(chips, 2 * down_rows, width)
    down_messages = pick_blocks(grad_down, sources)
    down_parts = plane_first(down_messages)

    unit_grads = [
        low(product_tn(after(normed_both, *down_messages), part)).reshape(chips, 2, 2 * rows, half)
        for part in (grad_gate, grad_up)
    ]

    def of_parity(which):
        picked = [lax.dynamic_index_in_dim(g, which, 1, keepdims=False) for g in unit_grads]
        return jnp.concatenate(picked, axis=2)

    unit_sent = of_parity(1 - y)
    unit_other = ring_turn(unit_sent)
    norm_part = product_nt(grad_gate, unit_w[:, :half]) + product_nt(grad_up, unit_w[:, half:])
    grad_norm = own_rows_sum(norm_part)
    unit_blocks = low(wide(of_parity(y)) + wide(unit_other))

    grad_gain = jnp.sum(grad_norm * scaled, axis=0)
    weighted = grad_norm * gain
    grad_hidden = (
        grad_out
        + inv_rms * weighted
        - scaled * inv_rms * inv_rms * jnp.mean(weighted * hidden, axis=-1, keepdims=True)
    )
    grad_mix = low(grad_hidden)
    mix_both = jnp.concatenate([grad_mix, core_swap(grad_mix)], axis=0)
    grad_conv_out = product_nt(mix_both, out_w)
    grad_out_w = low(product_tn(conv_low, mix_both))
    grad_c = grad_conv_out * convolved
    grad_conv = grad_conv_out * c_branch
    grad_mixed, grad_taps = conv_backward(grad_conv, mixed, taps, matches)
    grad_proj = low(jnp.concatenate([grad_mixed * x_branch, grad_c, grad_mixed * b_branch], axis=1))
    grad_in = low(product_tn(tokens_both, grad_proj))

    core_taps = jnp.stack(grad_taps, axis=0).reshape(tap_count, -1, 1, rows)
    is_core = lax.broadcasted_iota(jnp.int32, (1, 1, 2, 1), 2) == core
    grad_small = jnp.where(is_core, core_taps, 0.0).reshape(tap_count, width)
    grad_small = jnp.concatenate([grad_small, grad_gain[None]], axis=0)
    grad_small = jnp.pad(low(grad_small), ((0, AUX - tap_count - 1), (0, 0))).T
    out_blocks = grad_out_w.reshape(chips * 2, rows, width)
    out_blocks = jnp.concatenate([out_blocks[..., :lanes], out_blocks[..., lanes:]], axis=1)
    mix_blocks = jnp.concatenate([grad_in, grad_small, out_blocks.reshape(width, lanes)], axis=1)
    mix_blocks = after(mix_blocks.reshape(chips, SIDE * rows, mix_columns), unit_sent)
    mix_messages = pick_blocks(mix_blocks, sources)
    mix_parts = plane_first(mix_messages)

    unit_messages = pick_blocks(after(unit_blocks, *mix_messages), sources)
    ffn_out = own_rows_sum(ffn_part)
    block_out = low((hidden + ffn_out) * live_float)

    mix_parts = [after(part, unit_other) for part in mix_parts]
    down_sum = low(sum_wide(plane_second(down_parts, z, x, core)))
    input_part = product_nt(after(grad_proj, *unit_messages), in_w)
    input_grad = grad_hidden + own_rows_sum(input_part)
    down_sum = after(down_sum, *unit_messages)
    total_down = sum_wide(ring_parts(down_sum.reshape(2, down_rows, width), y))

    unit_parts = plane_first(unit_messages)
    unit_sum = low(sum_wide(plane_second(unit_parts, z, x, core))).reshape(2, rows, 2 * half)
    own = lax.dynamic_index_in_dim(unit_sum, core, 0, keepdims=False)
    other = lax.dynamic_index_in_dim(unit_sum, 1 - core, 0, keepdims=False)
    own_units = wide(own) + wide(ring_shift(own, 2))
    other_units = wide(ring_shift(other, 0, 1)) + wide(ring_shift(other, 2, 1))
    unit_zero = jnp.where(core == 0, own_units, other_units)
    unit_one = jnp.where(core == 0, other_units, own_units)

    def merge(first, second):
        pair = [part.reshape(rows, -1, down_rows) for part in (first, second)]
        return jnp.stack(pair, axis=2).reshape(rows, hidden_units)

    total_gate = merge(unit_zero[:, :half], unit_one[:, :half])
    total_up = merge(unit_zero[:, half:], unit_one[:, half:])

    mix_sum = low(sum_wide(plane_second(mix_parts, z, x, core)))
    mix_terms = ring_parts(mix_sum.reshape(2, 2 * rows, mix_columns), y)

    def mix_total(start, size):
        return sum_wide([lax.slice_in_dim(term, start, start + size, axis=1) for term in mix_terms])

    in_total = mix_total(0, in_columns + AUX).reshape(2, rows, in_columns + AUX)
    own_in = lax.dynamic_index_in_dim(in_total, core, 0, keepdims=False)
    other_in = core_swap(lax.dynamic_index_in_dim(in_total, 1 - core, 0, keepdims=False))
    halves = [part[:, :in_columns].reshape(rows, 3, -1, rows) for part in (own_in, other_in)]
    in_zero = jnp.where(core == 0, halves[0], halves[1])
    in_one = jnp.where(core == 0, halves[1], halves[0])
    total_in = jnp.stack([in_zero, in_one], axis=3).reshape(rows, 3 * width)
    out_total = mix_total(in_columns + AUX, lanes)
    total_out = jnp.concatenate([out_total[:rows], out_total[rows:]], axis=1)
    total_small = own_in[:, in_columns:] + other_in[:, in_columns:]
    lane = lax.broadcasted_iota(jnp.int32, total_small.shape, 1)
    small_columns = [
        jnp.sum(jnp.where(lane == k, total_small, 0.0), axis=1) for k in range(tap_count + 1)
    ]
    gradients = (
        total_in,
        jnp.stack(small_columns[:tap_count], axis=1),
        total_out,
        small_columns[tap_count],
        total_gate,
        total_up,
        total_down,
    )
    bias_one = 1.0 - BETA_ONE**STEP
    bias_two = 1.0 - BETA_TWO**STEP
    updated = []
    firsts = []
    seconds = []
    for master, moment, variance, gradient, step_rate, decay_rate in zip(
        masters, moments, squares, gradients, STEP_RATES, DECAY_RATES
    ):
        first_new = BETA_ONE * moment + (1.0 - BETA_ONE) * gradient
        second_new = BETA_TWO * variance + (1.0 - BETA_TWO) * gradient * gradient
        normalized = first_new / bias_one / (jnp.sqrt(second_new / bias_two) + ADAM_EPS)
        updated.append(master - step_rate * (normalized + decay_rate * master))
        firsts.append(first_new)
        seconds.append(second_new)
    return (block_out, input_grad, *updated, *firsts, *seconds)


def solution(mesh):
    grid = Mesh(mesh.devices.reshape(2, SIDE, SIDE, 2, 2), AXES)
    by_token = P(AXES, None)
    matrix, vector = P(SHARD, None), P(SHARD)
    group = (matrix, matrix, matrix, vector, matrix, matrix, matrix)
    return jax.shard_map(
        body,
        mesh=grid,
        in_specs=(by_token, by_token, P(), P(), *group, *group, *group),
        out_specs=(by_token, by_token, *group, *group, *group),
        check_vma=False,
    )
```
